32 devices in a mesh: seq: 4 (over x, core), dp: 8 (over z, y).
Axes of the slice: x: 2, y: 2, z: 4, core: 2. Of those that a mesh axis runs over, the one named last changes fastest.
Arguments:
- queries: bfloat16 [8, 512, 4096], P('dp', 'seq'), may hold values from -6 to 6
- keys: bfloat16 [8, 512, 512], P('dp', 'seq'), may hold values from -6 to 6
- values: bfloat16 [8, 512, 512], P('dp', 'seq'), may hold values from -6 to 6
- grad_out: bfloat16 [8, 512, 4096], P('dp', 'seq'), may hold values from -6 to 6
- features: bfloat16 [8, 512, 4096], P('dp', 'seq'), may hold values from -100 to 100
- doc_lengths: int32 [8, 8], P('dp'), may hold values from 1 to 128, 512 in all within a row
Outputs:
- key_grad: bfloat16 [8, 512, 512], P('dp', 'seq')
- clipped_grad: float32 [4096, 512], P(('seq', 'dp'))
The draws below stay inside these ranges and needn't reach their ends.
Inputs may be any that keep to these rules, and one draw needn't show every extreme that they name: `doc_lengths`: each row sums to 512; the longest document of every data group has exactly 128 tokens.
All inputs are finite; a program needn't handle non-finite values.
Results may differ from the reference program's by a relative error of at most 0.0058.
Values may be sent and summed in bfloat16 or wider, within the bound.
No kernel may reach another device: no remote copies, remote signals or barrier semaphores. Data moves between devices by JAX's collectives and lax.ppermute only.
A program may use at most 64 MiB of HBM per device.

```python
import math
import jax
import jax.numpy as jnp
import numpy as np
from jax import lax

HD = 128
HQ = 32
KVH = 4
DW = 4096
DOC_MAX = 128
QBLK = 512
SEQ_LEN = 512
NDOC = 8
N_SEQ = 4
N_DP = 8


def drawn_pair(key):
    base_seed = jax.random.fold_in(key, 11)
    query_seed = jax.random.fold_in(base_seed, 1)
    key_seed = jax.random.fold_in(base_seed, 2)
    query_drawn = jnp.clip(jax.random.normal(query_seed, (N_DP, SEQ_LEN, HQ * HD), jnp.float32), -4.0, 4.0)
    key_drawn = jnp.clip(jax.random.normal(key_seed, (N_DP, SEQ_LEN, KVH * HD), jnp.float32), -4.0, 4.0)
    return (query_drawn, key_drawn)


def value_pair(key):
    base_seed = jax.random.fold_in(key, 31)
    value_seed = jax.random.fold_in(base_seed, 1)
    noise_seed = jax.random.fold_in(base_seed, 2)
    value_drawn = jnp.clip(jax.random.normal(value_seed, (N_DP, SEQ_LEN, KVH * HD), jnp.float32), -4.0, 4.0)
    noise_drawn = jnp.clip(jax.random.normal(noise_seed, (N_DP, SEQ_LEN, HQ * HD), jnp.float32), -4.0, 4.0)
    value_four = value_drawn.reshape(N_DP, SEQ_LEN, KVH, HD)
    shared_heads = jnp.repeat(value_four, HQ // KVH, axis=2).reshape(N_DP, SEQ_LEN, HQ * HD)
    grad_drawn = 0.6 * shared_heads + 0.8 * noise_drawn
    return (value_drawn, grad_drawn)


def draw_queries(key, part):
    return drawn_pair(key)[0].astype(jnp.bfloat16)


def draw_keys(key, part):
    return drawn_pair(key)[1].astype(jnp.bfloat16)


def draw_values(key, part):
    return value_pair(key)[0].astype(jnp.bfloat16)


def draw_grad_out(key, part):
    return value_pair(key)[1].astype(jnp.bfloat16)


def draw_features(key, part):
    normal_seed = jax.random.fold_in(key, 21)
    column_seed = jax.random.fold_in(key, 22)
    row_seed = jax.random.fold_in(key, 23)
    offset_seed = jax.random.fold_in(key, 24)
    normal_part = jnp.clip(jax.random.normal(normal_seed, (N_DP, SEQ_LEN, DW), jnp.float32), -3.0, 3.0)
    column_rise = 3.0 ** (0.5 * jnp.arange(DW, dtype=jnp.float32) / DW)
    column_scale = 0.1 * 10.0 ** jax.random.uniform(column_seed, (DW,), jnp.float32) * column_rise
    row_scale = 10.0 ** jax.random.uniform(row_seed, (N_DP, SEQ_LEN, 1), jnp.float32)
    column_offset = 3.0 * (2 * jax.random.randint(offset_seed, (DW,), 0, 2) - 1).astype(jnp.float32)
    query_drawn = drawn_pair(key)[0]
    query_index = (jnp.arange(DW, dtype=jnp.int32) % (HQ * HD)).astype(jnp.int32)
    query_part = jnp.take(query_drawn, query_index, axis=2)
    mixed = normal_part * row_scale + 1.5 * query_part + column_offset
    return (mixed * column_scale).astype(jnp.bfloat16)


def length_profile(count, total, most, skew):
    weights = [(1 << 20) // math.isqrt(standing ** skew) + 1 for standing in range(2, count + 1)]
    rest, given = total - most - (count - 1), [1] * (count - 1)
    while rest > 0:
        free = [i for i in range(count - 1) if given[i] < most]
        whole, left = sum([weights[i] for i in free]), rest
        for i in free:
            addition = min(most - given[i], max(1, left * weights[i] // whole), rest)
            given[i] = given[i] + addition
            rest = rest - addition
    return np.array([most] + given)


def uneven_parts(own_key, amount, total, bound, lean):
    if amount == 2:
        one = jax.random.randint(own_key, (), max(1, total - bound), min(bound, total - 1) + 1)
        return jnp.stack([one, total - one])
    sizes = jnp.asarray(length_profile(amount, total, bound, lean), jnp.int32)
    pairs = (amount - 1) // 2
    donor, taker = sizes[1:1 + 2 * pairs:2], sizes[2:2 + 2 * pairs:2]
    margin = jnp.minimum(donor - 1, bound - taker)
    shifted = jax.random.randint(jax.random.fold_in(own_key, 1), (pairs,), 0, 1 << 20) % (margin + 1)
    sizes = sizes.at[1:1 + 2 * pairs:2].set(donor - shifted).at[2:2 + 2 * pairs:2].set(taker + shifted)
    return sizes[jax.random.permutation(jax.random.fold_in(own_key, 2), amount)]


def setup_inputs(seed: int = 0) -> dict:
    arg_keys = jax.random.split(jax.random.key(seed), 7)
    queries = draw_queries(jax.random.fold_in(arg_keys[6], 71), 0)
    keys = draw_keys(jax.random.fold_in(arg_keys[6], 71), 0)
    values = draw_values(jax.random.fold_in(arg_keys[6], 71), 0)
    grad_out = draw_grad_out(jax.random.fold_in(arg_keys[6], 71), 0)
    features = draw_features(jax.random.fold_in(arg_keys[6], 71), 0)
    doc_lengths = jax.vmap(lambda own: uneven_parts(own, NDOC, SEQ_LEN, DOC_MAX, 1))(jax.random.split(arg_keys[5], N_DP)).reshape((N_DP, NDOC)).astype(jnp.int32)
    return {"queries": queries, "keys": keys, "values": values, "grad_out": grad_out, "features": features, "doc_lengths": doc_lengths}


NEG_FILL = -1e+30

def doc_index(lengths, positions):
    doc_ends = jnp.cumsum(lengths, dtype=jnp.int32)
    located = lax.optimization_barrier(jnp.sum((doc_ends[None, :] <= positions[:, None]).astype(jnp.int32), axis=1))
    return jnp.where(positions < 0, -1, located).astype(jnp.int32)

def group_keys(group_pair):
    queries, keys, values, grad_out, lengths = group_pair
    slab_len = queries.shape[0]
    group_size = HQ // KVH
    sharers = N_SEQ // KVH
    local_heads = HQ // N_SEQ
    score_scale = 1.0 / math.sqrt(HD)
    block_width = QBLK + DOC_MAX
    query_four = queries.reshape(slab_len, KVH, group_size, HD).astype(jnp.float32)
    grad_four = grad_out.reshape(slab_len, KVH, group_size, HD).astype(jnp.float32)
    key_pad = jnp.concatenate([jnp.zeros((DOC_MAX, KVH, HD), jnp.float32), keys.reshape(slab_len, KVH, HD).astype(jnp.float32)], axis=0)
    value_pad = jnp.concatenate([jnp.zeros((DOC_MAX, KVH, HD), jnp.float32), values.reshape(slab_len, KVH, HD).astype(jnp.float32)], axis=0)

    def one_block(block_index, key_total):
        row_start = (block_index * QBLK).astype(jnp.int32)
        query_rows = lax.dynamic_slice_in_dim(query_four, row_start, QBLK, 0)
        grad_rows = lax.dynamic_slice_in_dim(grad_four, row_start, QBLK, 0)
        key_window = lax.dynamic_slice_in_dim(key_pad, row_start, block_width, 0)
        value_window = lax.dynamic_slice_in_dim(value_pad, row_start, block_width, 0)
        query_pos = row_start + jnp.arange(QBLK, dtype=jnp.int32)
        key_pos = row_start - DOC_MAX + jnp.arange(block_width, dtype=jnp.int32)
        query_doc = doc_index(lengths, query_pos)
        key_doc = doc_index(lengths, key_pos)
        visible = (query_doc[:, None] == key_doc[None, :]) & (key_pos[None, :] <= query_pos[:, None])
        scores = jnp.einsum('qrgd,krd->rgqk', query_rows, key_window, precision=lax.Precision.HIGHEST) * score_scale
        scores = jnp.where(visible[None, None], scores, NEG_FILL)
        row_peak = lax.optimization_barrier(jnp.max(scores, axis=3, keepdims=True))
        exponent = jnp.exp(scores - row_peak)
        attention = exponent / lax.optimization_barrier(jnp.sum(exponent, axis=3, keepdims=True))
        grad_weights = jnp.einsum('qrgd,krd->rgqk', grad_rows, value_window, precision=lax.Precision.HIGHEST)
        row_delta = lax.optimization_barrier(jnp.sum(attention * grad_weights, axis=3, keepdims=True))
        grad_scores = (attention * (grad_weights - row_delta) * score_scale).astype(jnp.bfloat16)
        grad_scores = lax.optimization_barrier(grad_scores).astype(jnp.float32)
        contribution = jnp.einsum('rgqk,qrgd->krgd', grad_scores, query_rows, precision=lax.Precision.HIGHEST)
        current = lax.dynamic_slice_in_dim(key_total, row_start, block_width, 0)
        return lax.dynamic_update_slice_in_dim(key_total, current + contribution, row_start, 0)
    key_total = lax.fori_loop(0, slab_len // QBLK, one_block, jnp.zeros((DOC_MAX + slab_len, KVH, group_size, HD), jnp.float32))
    device_parts = key_total[DOC_MAX:].reshape(slab_len, KVH, sharers, local_heads, HD).sum(axis=3)
    device_parts = lax.optimization_barrier(device_parts.astype(jnp.bfloat16)).astype(jnp.float32)
    return lax.optimization_barrier(jnp.sum(device_parts, axis=2)).reshape(slab_len, KVH * HD).astype(jnp.bfloat16)

def reference(queries, keys, values, grad_out, features, doc_lengths):
    key_grad = lax.map(group_keys, (queries, keys, values, grad_out, doc_lengths))

    def add_group(running, group_pair):
        group_features, group_grads = group_pair
        return (running + jnp.dot(group_features.T, group_grads, preferred_element_type=jnp.float32), None)
    weight_grad, unused = lax.scan(add_group, jnp.zeros((DW, KVH * HD), jnp.float32), (features, key_grad))
    root_mean = jnp.sqrt(jnp.mean(weight_grad * weight_grad) + 1e-06)
    clipped_grad = weight_grad * jnp.minimum(1.0, 1.0 / root_mean)
    return (key_grad, clipped_grad)
```

```python
import functools
import math

import jax
import jax.numpy as jnp
from jax import lax
from jax.experimental import pallas as pl
from jax.experimental.pallas import tpu as pltpu
from jax.sharding import PartitionSpec as P

HD = 128
HQ = 32
KVH = 4
DW = 4096
GROUP = HQ // KVH

NEG_FILL = -1e30
AXES = ("seq", "dp")
F32 = jnp.float32
BF16 = jnp.bfloat16
CORES = 2
HALF = KVH // CORES
WIDE = HALF * HD
SMEM = pl.BlockSpec(memory_space=pltpu.SMEM)


def params():
    return pltpu.CompilerParams(vmem_limit_bytes=40 << 20)


def cost(flops, moved, exps=0):
    return pl.CostEstimate(flops=flops, bytes_accessed=moved, transcendentals=exps)


def attention_kernel(pair, place, lengths, q, g, k_prev, k_own, v_prev, v_own, out, bias):
    rows = q.shape[0]

    @pl.when(pl.program_id(0) == 0)
    def _():
        base = place[0] * rows
        query_pos = base + lax.broadcasted_iota(jnp.int32, (1, rows), 1)
        start = jnp.zeros((1, rows), jnp.int32)
        end = jnp.int32(0)
        for d in range(lengths.shape[1]):
            end = end + lengths[0, d]
            start = jnp.where(end <= query_pos, end, start)
        key_pos = base - rows + lax.broadcasted_iota(jnp.int32, (2 * rows, rows), 0)
        visible = (key_pos >= start) & (key_pos <= query_pos)
        one = jnp.where(visible, 0.0, NEG_FILL).astype(F32)
        for n in range(pair):
            bias[:, n * rows : (n + 1) * rows] = one

    key = jnp.concatenate([k_prev[...], k_own[...]], axis=0)
    value = jnp.concatenate([v_prev[...], v_own[...]], axis=0)
    scale = 1.0 / math.sqrt(HD)
    scale2 = scale * math.log2(math.e)
    nt = (((1,), (1,)), ((), ()))
    nn = (((1,), (0,)), ((), ()))
    total = None
    for h in range(0, GROUP, pair):
        heads = [slice((h + n) * HD, (h + n + 1) * HD) for n in range(pair)]
        q_rows = jnp.concatenate([q[:, head] for head in heads], axis=0)
        g_rows = jnp.concatenate([g[:, head] for head in heads], axis=0)
        scores = lax.dot_general(key, q_rows, nt, preferred_element_type=F32)
        weights = lax.dot_general(value, g_rows, nt, preferred_element_type=F32)
        scores = scores * scale2 + bias[...]
        exponent = jnp.exp2(scores - jnp.max(scores, axis=0, keepdims=True))
        inverse = 1.0 / jnp.sum(exponent, axis=0, keepdims=True)
        delta = jnp.sum(exponent * weights, axis=0, keepdims=True) * inverse
        grads = ((exponent * (inverse * scale)) * (weights - delta)).astype(BF16)
        part = lax.dot_general(grads, q_rows, nn, preferred_element_type=F32)
        total = part if total is None else total + part
    out[0] = total.astype(out.dtype)


def attention(place, lengths, q, g, k_prev, k_own, v_prev, v_own, heads, dtype):
    rows = q.shape[0]
    head = lambda i, p, l: (0, p[1] + i)
    size = heads * 2 * rows * GROUP * rows
    return pl.pallas_call(
        functools.partial(attention_kernel, 4),
        grid_spec=pltpu.PrefetchScalarGridSpec(
            num_scalar_prefetch=2,
            grid=(heads,),
            in_specs=[pl.BlockSpec((rows, GROUP * HD), head)] * 2
            + [pl.BlockSpec((rows, HD), head)] * 4,
            out_specs=pl.BlockSpec((1, 2 * rows, HD), lambda i, p, l: (i, 0, 0)),
            scratch_shapes=[pltpu.VMEM((2 * rows, 4 * rows), F32)],
        ),
        out_shape=jax.ShapeDtypeStruct((heads, 2 * rows, HD), dtype),
        compiler_params=params(),
        cost_estimate=cost(6 * size * HD, heads * rows * GROUP * HD * 4, size),
    )(place, lengths, q, g, k_prev, k_own, v_prev, v_own)


def pack_kernel(sizes, x_ref, out):
    nx, ny, nz = sizes
    block = DW // (nx * CORES * ny * nz)
    for x in range(nx):
        for y in range(ny):
            for z in range(nz):
                for c in range(CORES):
                    source = ((x * CORES + c) * nz + z) * ny + y
                    out[x * ny + y, z, :, c * block : (c + 1) * block] = x_ref[
                        :, source * block : (source + 1) * block
                    ]


def pack(features, sizes):
    nx, ny, nz = sizes
    rows = features.shape[0]
    shape = (nx * ny, nz, rows, DW // (nx * ny * nz))
    return pl.pallas_call(
        functools.partial(pack_kernel, sizes),
        out_shape=jax.ShapeDtypeStruct(shape, BF16),
        compiler_params=params(),
        cost_estimate=cost(0, 2 * rows * DW * 2),
    )(features)


def merge_kernel(place, mine, theirs, out):
    rows = mine.shape[1] // 2

    def write(even, odd):
        for h in range(HALF):
            cols = slice(h * HD, (h + 1) * HD)
            out[:rows, cols] = even[h, :rows]
            out[rows : 2 * rows, cols] = (
                even[h, rows:].astype(F32) + odd[h, :rows].astype(F32)
            ).astype(BF16)
            out[2 * rows :, cols] = odd[h, rows:]

    @pl.when(place[0] == 0)
    def _():
        write(mine, theirs)

    @pl.when(place[0] == 1)
    def _():
        write(theirs, mine)


def merge(place, mine, theirs):
    rows = mine.shape[1] // 2
    vmem = pl.BlockSpec(memory_space=pltpu.VMEM)
    return pl.pallas_call(
        merge_kernel,
        in_specs=[SMEM, vmem, vmem],
        out_specs=vmem,
        out_shape=jax.ShapeDtypeStruct((3 * rows, WIDE), BF16),
        compiler_params=params(),
        cost_estimate=cost(rows * WIDE, 7 * rows * WIDE * 2),
    )(place, mine, theirs)


def weight_kernel(nz, place, g0, g1, g2, g3, f_same, f_other, *rest):
    sends, (keep, key_mine, key_theirs, same, other) = rest[: nz - 1], rest[nz - 1 :]
    rows = g0.shape[0] // 3
    core, chip, z = place[0], place[1], place[2]
    chips = (g0, g1, g2, g3)
    for m in range(4):
        even = chips[m][rows : 2 * rows]
        odd = (chips[m][2 * rows :].astype(F32) + chips[m ^ 2][:rows].astype(F32)).astype(BF16)
        at = pl.ds(pl.multiple_of((chip ^ m) * rows, rows), rows)
        own = jnp.where(core == 0, even, odd)
        far = jnp.where(core == 0, odd, even)
        same[at] = own
        other[at] = far
        if m == 0:
            key_mine[...] = own
            key_theirs[...] = far
    tn = (((0,), (0,)), ((), ()))
    for m in (2, 3, 1, 0):
        block = z ^ m
        left = f_same[:, pl.ds(block, 1)].reshape(4 * rows, WIDE)
        right = f_other[:, pl.ds(block, 1)].reshape(4 * rows, WIDE)
        product = lax.dot_general(same[...], left, tn, preferred_element_type=F32)
        product += lax.dot_general(other[...], right, tn, preferred_element_type=F32)
        if m == 0:
            keep[...] = product
        else:
            sends[m - 1][...] = product.astype(BF16)


def weight(place, chips, f_same, f_other):
    rows = chips[0].shape[0] // 3
    nz = f_same.shape[1]
    vmem = pl.BlockSpec(memory_space=pltpu.VMEM)
    square = (WIDE, f_same.shape[3])
    shapes = [jax.ShapeDtypeStruct(square, BF16)] * (nz - 1)
    shapes += [jax.ShapeDtypeStruct(square, F32)] + [jax.ShapeDtypeStruct((rows, WIDE), BF16)] * 2
    return pl.pallas_call(
        functools.partial(weight_kernel, nz),
        in_specs=[SMEM] + [vmem] * 6,
        out_specs=[vmem] * len(shapes),
        out_shape=shapes,
        scratch_shapes=[pltpu.VMEM((4 * rows, WIDE), BF16)] * 2,
        compiler_params=params(),
        cost_estimate=cost(2 * 8 * rows * WIDE * 4 * WIDE, 4 << 20),
    )(place, *chips, f_same, f_other)


def reduce_kernel(place, keep, r1, r2, r3, mine, theirs, squares):
    total = keep[...] + r1[...].astype(F32) + r2[...].astype(F32) + r3[...].astype(F32)
    half = total.shape[1] // 2
    low, high = total[:, :half], total[:, half:]
    mine[...] = jnp.where(place[0] == 0, low, high)
    theirs[...] = jnp.where(place[0] == 0, high, low)
    sums = jnp.sum(low * low + high * high, axis=0, keepdims=True)
    squares[...] = jnp.broadcast_to(sums[None], squares.shape)


def reduce_planes(place, keep, received, devices):
    cols, both = keep.shape
    vmem = pl.BlockSpec(memory_space=pltpu.VMEM)
    half = jax.ShapeDtypeStruct((cols, both // 2), F32)
    return pl.pallas_call(
        reduce_kernel,
        in_specs=[SMEM] + [vmem] * 4,
        out_specs=[vmem] * 3,
        out_shape=[half, half, jax.ShapeDtypeStruct((devices, 1, both // 2), F32)],
        compiler_params=params(),
        cost_estimate=cost(8 * cols * both, cols * both * 14),
    )(place, keep, *received)


def finish_kernel(place, squares, mine, theirs, key_mine, key_theirs, key_out, out):
    entries = DW * KVH * HD
    total = jnp.sum(jnp.sum(squares[...], axis=0, keepdims=True), axis=2, keepdims=True)
    root_mean = jnp.sqrt(total / entries + 1e-06)
    factor = jnp.minimum(1.0, 1.0 / root_mean)[0]
    first = place[0] == 0
    low = (mine[...] * factor).T
    high = (theirs[...] * factor).T
    out[:, :WIDE] = jnp.where(first, low, high)
    out[:, WIDE:] = jnp.where(first, high, low)
    key_out[0, :, :WIDE] = jnp.where(first, key_mine[...], key_theirs[...])
    key_out[0, :, WIDE:] = jnp.where(first, key_theirs[...], key_mine[...])


def finish(place, squares, mine, theirs, key_mine, key_theirs):
    rows = key_mine.shape[0]
    vmem = pl.BlockSpec(memory_space=pltpu.VMEM)
    return pl.pallas_call(
        finish_kernel,
        in_specs=[SMEM] + [vmem] * 5,
        out_specs=[vmem] * 2,
        out_shape=[
            jax.ShapeDtypeStruct((1, rows, KVH * HD), BF16),
            jax.ShapeDtypeStruct((mine.shape[1], KVH * HD), F32),
        ],
        compiler_params=params(),
        cost_estimate=cost(4 * rows * KVH * HD, 4 * rows * KVH * HD * 4),
    )(place, squares, mine, theirs, key_mine, key_theirs)


def planes(queries, keys, values, grad_out, features, doc_lengths):
    seq_count, dp_count = lax.axis_size("seq"), lax.axis_size("dp")
    devices = seq_count * dp_count
    nx, ny = seq_count // CORES, 2
    nz = dp_count // ny
    seq, dp = lax.axis_index("seq"), lax.axis_index("dp")
    core, x, y, z = seq % CORES, seq // CORES, dp % ny, dp // ny
    as_place = lambda *items: jnp.stack([jnp.asarray(i, jnp.int32) for i in items])

    def swap(array, mask):
        return lax.ppermute(array, AXES, [(i, i ^ mask) for i in range(devices)])

    core_mask, x_mask, y_mask, z_mask = dp_count, CORES * dp_count, 1, ny
    following = [(i, (i + 1) % seq_count) for i in range(seq_count)]
    k_own, v_own = keys[0], values[0]
    k_prev = lax.ppermute(k_own, "seq", following)
    v_prev = lax.ppermute(v_own, "seq", following)

    packed = pack(features[0], (nx, ny, nz))
    members = [
        [
            ((a * CORES + c) * nz + b) * ny + e
            for a in range(nx)
            for e in range(ny)
        ]
        for c in range(CORES)
        for b in range(nz)
    ]
    f_same = lax.all_to_all(packed, AXES, 0, 0, axis_index_groups=members, tiled=True)
    f_other = swap(f_same, core_mask)

    near = (queries[0], grad_out[0], k_prev, k_own, v_prev, v_own)
    to_send = attention(as_place(seq, (1 - core) * HALF), doc_lengths, *near, HALF, BF16)
    theirs = swap(to_send, core_mask)
    mine = attention(as_place(seq, core * HALF), doc_lengths, *near, HALF, BF16)
    place = as_place(core, x * ny + y, z)
    chip = merge(place, mine, theirs)
    chips = [chip, swap(chip, y_mask), swap(chip, x_mask), swap(chip, x_mask + y_mask)]

    *sends, keep, key_mine, key_send = weight(place, chips, f_same, f_other)
    received = [swap(part, (m + 1) * z_mask) for m, part in enumerate(sends)]
    key_other = swap(key_send, core_mask)
    rows_mine, rows_send, squares = reduce_planes(place, keep, received, devices)
    rows_other = swap(rows_send, core_mask)
    squares = lax.all_to_all(squares, AXES, 0, 0, tiled=True)
    return finish(place, squares, rows_mine, rows_other, key_mine, key_other)


def rings(queries, keys, values, grad_out, features, doc_lengths):
    seq_count = lax.axis_size("seq")
    rows = queries.shape[1]
    following = [(i, (i + 1) % seq_count) for i in range(seq_count)]
    preceding = [(i, (i - 1) % seq_count) for i in range(seq_count)]
    k_own, v_own = keys[0], values[0]
    k_prev = lax.ppermute(k_own, "seq", following)
    v_prev = lax.ppermute(v_own, "seq", following)
    seq = lax.axis_index("seq")
    place = jnp.stack([seq, jnp.zeros_like(seq)]).astype(jnp.int32)
    near = (queries[0], grad_out[0], k_prev, k_own, v_prev, v_own)
    parts = attention(place, doc_lengths, *near, KVH, F32)
    parts = parts.transpose(1, 0, 2).reshape(2 * rows, KVH * HD)
    after = lax.ppermute(parts[:rows], "seq", preceding)
    key_grad = (parts[rows:] + after).astype(BF16)
    columns = lax.all_to_all(features[0], "seq", split_axis=1, concat_axis=0, tiled=True)
    weight_part = lax.dot_general(
        columns,
        lax.all_gather(key_grad, "seq", axis=0, tiled=True),
        (((0,), (0,)), ((), ())),
        preferred_element_type=F32,
    )
    own_rows = lax.psum_scatter(weight_part, "dp", scatter_dimension=0, tiled=True)
    squares = lax.psum(jnp.sum(own_rows * own_rows), AXES)
    root_mean = jnp.sqrt(squares / (DW * KVH * HD) + 1e-06)
    return (key_grad[None], own_rows * jnp.minimum(1.0, 1.0 / root_mean))


def solution(mesh):
    in_specs = (
        P("dp", "seq", None),
        P("dp", "seq", None),
        P("dp", "seq", None),
        P("dp", "seq", None),
        P("dp", "seq", None),
        P("dp", None),
    )
    out_specs = (P("dp", "seq", None), P(("seq", "dp"), None))
    small = mesh.shape["seq"] == 2 * CORES and mesh.shape["dp"] == 8
    body = planes if small else rings
    return jax.shard_map(body, mesh=mesh, in_specs=in_specs, out_specs=out_specs, check_vma=False)
```

```python
import functools
import math

import jax
import jax.numpy as jnp
from jax import lax
from jax.experimental import pallas as pl
from jax.experimental.pallas import tpu as pltpu
from jax.sharding import PartitionSpec as P

HD = 128
HQ = 32
KVH = 4
DW = 4096
GROUP = HQ // KVH

NEG_FILL = -1e30
AXES = ("seq", "dp")
F32 = jnp.float32
BF16 = jnp.bfloat16
CORES = 2
HALF = KVH // CORES
WIDE = HALF * HD
SMEM = pl.BlockSpec(memory_space=pltpu.SMEM)


def params():
    return pltpu.CompilerParams(vmem_limit_bytes=40 << 20)


def cost(flops, moved, exps=0):
    return pl.CostEstimate(flops=flops, bytes_accessed=moved, transcendentals=exps)


def attention_kernel(pair, place, lengths, q, g, k_prev, k_own, v_prev, v_own, out, bias):
    rows = q.shape[0]

    @pl.when(pl.program_id(0) == 0)
    def _():
        base = place[0] * rows
        query_pos = base + lax.broadcasted_iota(jnp.int32, (1, rows), 1)
        start = jnp.zeros((1, rows), jnp.int32)
        end = jnp.int32(0)
        for d in range(lengths.shape[1]):
            end = end + lengths[0, d]
            start = jnp.where(end <= query_pos, end, start)
        key_pos = base - rows + lax.broadcasted_iota(jnp.int32, (2 * rows, rows), 0)
        visible = (key_pos >= start) & (key_pos <= query_pos)
        one = jnp.where(visible, 0.0, NEG_FILL).astype(F32)
        for n in range(pair):
            bias[:, n * rows : (n + 1) * rows] = one

    key = jnp.concatenate([k_prev[...], k_own[...]], axis=0)
    value = jnp.concatenate([v_prev[...], v_own[...]], axis=0)
    scale = 1.0 / math.sqrt(HD)
    scale2 = scale * math.log2(math.e)
    nt = (((1,), (1,)), ((), ()))
    nn = (((1,), (0,)), ((), ()))
    total = None
    for h in range(0, GROUP, pair):
        heads = [slice((h + n) * HD, (h + n + 1) * HD) for n in range(pair)]
        q_rows = jnp.concatenate([q[:, head] for head in heads], axis=0)
        g_rows = jnp.concatenate([g[:, head] for head in heads], axis=0)
        scores = lax.dot_general(key, q_rows, nt, preferred_element_type=F32)
        weights = lax.dot_general(value, g_rows, nt, preferred_element_type=F32)
        scores = scores * scale2 + bias[...]
        exponent = jnp.exp2(scores - jnp.max(scores, axis=0, keepdims=True))
        inverse = 1.0 / jnp.sum(exponent, axis=0, keepdims=True)
        delta = jnp.sum(exponent * weights, axis=0, keepdims=True) * inverse
        grads = ((exponent * (inverse * scale)) * (weights - delta)).astype(BF16)
        part = lax.dot_general(grads, q_rows, nn, preferred_element_type=F32)
        total = part if total is None else total + part
    out[0] = total.astype(out.dtype)


def attention(place, lengths, q, g, k_prev, k_own, v_prev, v_own, heads, dtype):
    rows = q.shape[0]
    head = lambda i, p, l: (0, p[1] + i)
    size = heads * 2 * rows * GROUP * rows
    return pl.pallas_call(
        functools.partial(attention_kernel, 4),
        grid_spec=pltpu.PrefetchScalarGridSpec(
            num_scalar_prefetch=2,
            grid=(heads,),
            in_specs=[pl.BlockSpec((rows, GROUP * HD), head)] * 2
            + [pl.BlockSpec((rows, HD), head)] * 4,
            out_specs=pl.BlockSpec((1, 2 * rows, HD), lambda i, p, l: (i, 0, 0)),
            scratch_shapes=[pltpu.VMEM((2 * rows, 4 * rows), F32)],
        ),
        out_shape=jax.ShapeDtypeStruct((heads, 2 * rows, HD), dtype),
        compiler_params=params(),
        cost_estimate=cost(6 * size * HD, heads * rows * GROUP * HD * 4, size),
    )(place, lengths, q, g, k_prev, k_own, v_prev, v_own)


def pack_kernel(sizes, place, x_ref, *outs):
    ny, nz = sizes
    block = outs[0].shape[2] // CORES
    x, y = place[1] // ny, place[1] % ny
    for m, out in enumerate(outs):
        for z in range(nz):
            for c in range(CORES):
                source = (((x ^ (m // ny)) * CORES + c) * nz + z) * ny + (y ^ (m % ny))
                at = pl.ds(pl.multiple_of(source * block, block), block)
                out[z, :, c * block : (c + 1) * block] = x_ref[:, at]


def pack(place, features, sizes):
    nx, ny, nz = sizes
    rows = features.shape[0]
    shape = jax.ShapeDtypeStruct((nz, rows, DW // (nx * ny * nz)), BF16)
    vmem = pl.BlockSpec(memory_space=pltpu.VMEM)
    return pl.pallas_call(
        functools.partial(pack_kernel, (ny, nz)),
        in_specs=[SMEM, vmem],
        out_specs=[vmem] * (nx * ny),
        out_shape=[shape] * (nx * ny),
        compiler_params=params(),
        cost_estimate=cost(0, 64 << 20),
    )(place, features)


def merge_kernel(place, mine, theirs, out):
    rows = mine.shape[1] // 2

    def write(even, odd):
        for h in range(HALF):
            cols = slice(h * HD, (h + 1) * HD)
            out[:rows, cols] = even[h, :rows]
            out[rows : 2 * rows, cols] = (
                even[h, rows:].astype(F32) + odd[h, :rows].astype(F32)
            ).astype(BF16)
            out[2 * rows :, cols] = odd[h, rows:]

    @pl.when(place[0] == 0)
    def _():
        write(mine, theirs)

    @pl.when(place[0] == 1)
    def _():
        write(theirs, mine)


def merge(place, mine, theirs):
    rows = mine.shape[1] // 2
    vmem = pl.BlockSpec(memory_space=pltpu.VMEM)
    return pl.pallas_call(
        merge_kernel,
        in_specs=[SMEM, vmem, vmem],
        out_specs=vmem,
        out_shape=jax.ShapeDtypeStruct((3 * rows, WIDE), BF16),
        compiler_params=params(),
        cost_estimate=cost(rows * WIDE, 7 * rows * WIDE * 2),
    )(place, mine, theirs)


def weight_kernel(nz, place, *refs):
    chips, f_same, f_other = refs[:4], refs[4:8], refs[8]
    sends, (keep, key_mine, key_theirs, same, other) = refs[9 : 8 + nz], refs[8 + nz :]
    rows = chips[0].shape[0] // 3
    core, z = place[0], place[2]
    for m in range(4):
        even = chips[m][rows : 2 * rows]
        odd = (chips[m][2 * rows :].astype(F32) + chips[m ^ 2][:rows].astype(F32)).astype(BF16)
        own = jnp.where(core == 0, even, odd)
        far = jnp.where(core == 0, odd, even)
        same[m * rows : (m + 1) * rows] = own
        other[m * rows : (m + 1) * rows] = far
        if m == 0:
            key_mine[...] = own
            key_theirs[...] = far
    tn = (((0,), (0,)), ((), ()))
    for m in (2, 3, 1, 0):
        left = jnp.concatenate([f[z ^ m] for f in f_same], axis=0)
        right = jnp.concatenate([f_other[n, z ^ m] for n in range(4)], axis=0)
        product = lax.dot_general(same[...], left, tn, preferred_element_type=F32)
        product += lax.dot_general(other[...], right, tn, preferred_element_type=F32)
        if m == 0:
            keep[...] = product
        else:
            sends[m - 1][...] = product.astype(BF16)


def weight(place, chips, f_same, f_other):
    rows = chips[0].shape[0] // 3
    nz = f_same[0].shape[0]
    vmem = pl.BlockSpec(memory_space=pltpu.VMEM)
    square = (WIDE, f_same[0].shape[2])
    shapes = [jax.ShapeDtypeStruct(square, BF16)] * (nz - 1)
    shapes += [jax.ShapeDtypeStruct(square, F32)] + [jax.ShapeDtypeStruct((rows, WIDE), BF16)] * 2
    return pl.pallas_call(
        functools.partial(weight_kernel, nz),
        in_specs=[SMEM] + [vmem] * 9,
        out_specs=[vmem] * len(shapes),
        out_shape=shapes,
        scratch_shapes=[pltpu.VMEM((4 * rows, WIDE), BF16)] * 2,
        compiler_params=params(),
        cost_estimate=cost(2 * 8 * rows * WIDE * 4 * WIDE, 4 << 20),
    )(place, *chips, *f_same, f_other)


def reduce_kernel(place, keep, r1, r2, r3, mine, theirs, squares):
    total = keep[...] + r1[...].astype(F32) + r2[...].astype(F32) + r3[...].astype(F32)
    half = total.shape[1] // 2
    low, high = total[:, :half], total[:, half:]
    mine[...] = jnp.where(place[0] == 0, low, high)
    theirs[...] = jnp.where(place[0] == 0, high, low)
    sums = jnp.sum(low * low + high * high, axis=0, keepdims=True)
    squares[...] = jnp.broadcast_to(sums[None], squares.shape)


def reduce_planes(place, keep, received, devices):
    cols, both = keep.shape
    vmem = pl.BlockSpec(memory_space=pltpu.VMEM)
    half = jax.ShapeDtypeStruct((cols, both // 2), F32)
    return pl.pallas_call(
        reduce_kernel,
        in_specs=[SMEM] + [vmem] * 4,
        out_specs=[vmem] * 3,
        out_shape=[half, half, jax.ShapeDtypeStruct((devices, 1, both // 2), F32)],
        compiler_params=params(),
        cost_estimate=cost(8 * cols * both, cols * both * 14),
    )(place, keep, *received)


def finish_kernel(place, squares, mine, theirs, key_mine, key_theirs, key_out, out):
    entries = DW * KVH * HD
    total = jnp.sum(jnp.sum(squares[...], axis=0, keepdims=True), axis=2, keepdims=True)
    root_mean = jnp.sqrt(total / entries + 1e-06)
    factor = jnp.minimum(1.0, 1.0 / root_mean)[0]
    first = place[0] == 0
    low = (mine[...] * factor).T
    high = (theirs[...] * factor).T
    out[:, :WIDE] = jnp.where(first, low, high)
    out[:, WIDE:] = jnp.where(first, high, low)
    key_out[0, :, :WIDE] = jnp.where(first, key_mine[...], key_theirs[...])
    key_out[0, :, WIDE:] = jnp.where(first, key_theirs[...], key_mine[...])


def finish(place, squares, mine, theirs, key_mine, key_theirs):
    rows = key_mine.shape[0]
    vmem = pl.BlockSpec(memory_space=pltpu.VMEM)
    return pl.pallas_call(
        finish_kernel,
        in_specs=[SMEM] + [vmem] * 5,
        out_specs=[vmem] * 2,
        out_shape=[
            jax.ShapeDtypeStruct((1, rows, KVH * HD), BF16),
            jax.ShapeDtypeStruct((mine.shape[1], KVH * HD), F32),
        ],
        compiler_params=params(),
        cost_estimate=cost(4 * rows * KVH * HD, 4 * rows * KVH * HD * 4),
    )(place, squares, mine, theirs, key_mine, key_theirs)


def planes(queries, keys, values, grad_out, features, doc_lengths):
    seq_count, dp_count = lax.axis_size("seq"), lax.axis_size("dp")
    devices = seq_count * dp_count
    nx, ny = seq_count // CORES, 2
    nz = dp_count // ny
    seq, dp = lax.axis_index("seq"), lax.axis_index("dp")
    core, x, y, z = seq & 1, seq >> 1, dp & 1, dp >> 1
    as_place = lambda *items: jnp.stack([jnp.asarray(i, jnp.int32) for i in items])

    def swap(array, mask):
        return lax.ppermute(array, AXES, [(i, i ^ mask) for i in range(devices)])

    core_mask, x_mask, y_mask, z_mask = dp_count, CORES * dp_count, 1, ny
    following = [(i, (i + 1) % seq_count) for i in range(seq_count)]
    k_own, v_own = keys[0], values[0]
    k_prev = lax.ppermute(k_own, "seq", following)
    v_prev = lax.ppermute(v_own, "seq", following)

    place = as_place(core, x * ny + y, z)
    masks = [0, y_mask, x_mask, x_mask + y_mask]
    packed = pack(place, features[0], (nx, ny, nz))
    f_same = [packed[0]] + [swap(part, mask) for part, mask in zip(packed[1:], masks[1:])]

    near = (queries[0], grad_out[0], k_prev, k_own, v_prev, v_own)
    to_send = attention(as_place(seq, (1 - core) * HALF), doc_lengths, *near, HALF, BF16)
    theirs = swap(to_send, core_mask)
    mine = attention(as_place(seq, core * HALF), doc_lengths, *near, HALF, BF16)
    chip = merge(place, mine, theirs)
    chips = [chip] + [swap(chip, mask) for mask in masks[1:]]
    f_ready, _ = lax.optimization_barrier((f_same, chip))
    f_other = swap(jnp.stack(f_ready), core_mask)

    *sends, keep, key_mine, key_send = weight(place, chips, f_same, f_other)
    received = [swap(sends[m], (m + 1) * z_mask) for m in (1, 2, 0)]
    key_other = swap(key_send, core_mask)
    rows_mine, rows_send, squares = reduce_planes(place, keep, received, devices)
    rows_other = swap(rows_send, core_mask)
    squares = lax.all_to_all(squares, AXES, 0, 0, tiled=True)
    return finish(place, squares, rows_mine, rows_other, key_mine, key_other)


def rings(queries, keys, values, grad_out, features, doc_lengths):
    seq_count = lax.axis_size("seq")
    rows = queries.shape[1]
    following = [(i, (i + 1) % seq_count) for i in range(seq_count)]
    preceding = [(i, (i - 1) % seq_count) for i in range(seq_count)]
    k_own, v_own = keys[0], values[0]
    k_prev = lax.ppermute(k_own, "seq", following)
    v_prev = lax.ppermute(v_own, "seq", following)
    seq = lax.axis_index("seq")
    place = jnp.stack([seq, jnp.zeros_like(seq)]).astype(jnp.int32)
    near = (queries[0], grad_out[0], k_prev, k_own, v_prev, v_own)
    parts = attention(place, doc_lengths, *near, KVH, F32)
    parts = parts.transpose(1, 0, 2).reshape(2 * rows, KVH * HD)
    after = lax.ppermute(parts[:rows], "seq", preceding)
    key_grad = (parts[rows:] + after).astype(BF16)
    columns = lax.all_to_all(features[0], "seq", split_axis=1, concat_axis=0, tiled=True)
    weight_part = lax.dot_general(
        columns,
        lax.all_gather(key_grad, "seq", axis=0, tiled=True),
        (((0,), (0,)), ((), ())),
        preferred_element_type=F32,
    )
    own_rows = lax.psum_scatter(weight_part, "dp", scatter_dimension=0, tiled=True)
    squares = lax.psum(jnp.sum(own_rows * own_rows), AXES)
    root_mean = jnp.sqrt(squares / (DW * KVH * HD) + 1e-06)
    return (key_grad[None], own_rows * jnp.minimum(1.0, 1.0 / root_mean))


def solution(mesh):
    in_specs = (
        P("dp", "seq", None),
        P("dp", "seq", None),
        P("dp", "seq", None),
        P("dp", "seq", None),
        P("dp", "seq", None),
        P("dp", None),
    )
    out_specs = (P("dp", "seq", None), P(("seq", "dp"), None))
    small = mesh.shape["seq"] == 2 * CORES and mesh.shape["dp"] == 8
    body = planes if small else rings
    return jax.shard_map(body, mesh=mesh, in_specs=in_specs, out_specs=out_specs, check_vma=False)
```

```python
import functools
import math

import jax
import jax.numpy as jnp
from jax import lax
from jax.experimental import pallas as pl
from jax.experimental.pallas import tpu as pltpu
from jax.sharding import PartitionSpec as P

HD = 128
HQ = 32
KVH = 4
DW = 4096
GROUP = HQ // KVH

NEG_FILL = -1e30
AXES = ("seq", "dp")
F32 = jnp.float32
BF16 = jnp.bfloat16
CORES = 2
HALF = KVH // CORES
WIDE = HALF * HD


def params(mib=40):
    return pltpu.CompilerParams(vmem_limit_bytes=mib << 20)


def cost(flops, moved, exps=0):
    return pl.CostEstimate(flops=flops, bytes_accessed=moved, transcendentals=exps)


def position():
    seq, dp = lax.axis_index("seq"), lax.axis_index("dp")
    return seq & 1, seq >> 1, dp & 1, dp >> 1


def first_head(which):
    if which is None:
        return 0
    core = lax.axis_index("seq") & 1
    return (core if which == 0 else 1 - core) * HALF


def attention_kernel(which, heads, lengths, q, g, k_prev, k_own, v_prev, v_own, out, *scratch):
    ends, q_buf, g_buf, k_buf, v_buf, bias, sems = scratch
    rows = q.shape[0]
    pair = bias.shape[1] // rows
    first = first_head(which)
    waits = [[] for _ in range(heads)]
    length_copy = pltpu.make_async_copy(lengths, ends, sems.at[6 * heads])
    length_copy.start()
    for h in range(heads):
        wide = pl.ds(pl.multiple_of((first + h) * GROUP * HD, GROUP * HD), GROUP * HD)
        one = pl.ds(pl.multiple_of((first + h) * HD, HD), HD)
        moves = [
            (k_prev.at[:, one], k_buf.at[h, :rows]),
            (k_own.at[:, one], k_buf.at[h, rows:]),
            (q.at[:, wide], q_buf.at[h]),
            (v_prev.at[:, one], v_buf.at[h, :rows]),
            (v_own.at[:, one], v_buf.at[h, rows:]),
            (g.at[:, wide], g_buf.at[h]),
        ]
        for n, (source, target) in enumerate(moves):
            copy = pltpu.make_async_copy(source, target, sems.at[6 * h + n])
            copy.start()
            waits[h].append(copy)
    length_copy.wait()
    base = lax.axis_index("seq") * rows
    query_pos = base + lax.broadcasted_iota(jnp.int32, (1, rows), 1)
    start = jnp.zeros((1, rows), jnp.int32)
    end = jnp.int32(0)
    for d in range(ends.shape[1]):
        end = end + ends[0, d]
        start = jnp.where(end <= query_pos, end, start)
    key_pos = base - rows + lax.broadcasted_iota(jnp.int32, (2 * rows, rows), 0)
    visible = (key_pos >= start) & (key_pos <= query_pos)
    hidden = jnp.where(visible, 0.0, NEG_FILL).astype(F32)
    for n in range(pair):
        bias[:, n * rows : (n + 1) * rows] = hidden

    scale = 1.0 / math.sqrt(HD)
    scale2 = scale * math.log2(math.e)
    nt = (((1,), (1,)), ((), ()))
    nn = (((1,), (0,)), ((), ()))
    for r in range(heads):
        for copy in waits[r]:
            copy.wait()
        key, value = k_buf[r], v_buf[r]
        total = None
        for h in range(0, GROUP, pair):
            cols = [slice((h + n) * HD, (h + n + 1) * HD) for n in range(pair)]
            q_rows = jnp.concatenate([q_buf[r, :, c] for c in cols], axis=0)
            g_rows = jnp.concatenate([g_buf[r, :, c] for c in cols], axis=0)
            scores = lax.dot_general(key, q_rows, nt, preferred_element_type=F32)
            weights = lax.dot_general(value, g_rows, nt, preferred_element_type=F32)
            scores = scores * scale2 + bias[...]
            exponent = jnp.exp2(scores - jnp.max(scores, axis=0, keepdims=True))
            inverse = 1.0 / jnp.sum(exponent, axis=0, keepdims=True)
            delta = jnp.sum(exponent * weights, axis=0, keepdims=True) * inverse
            grads = ((exponent * (inverse * scale)) * (weights - delta)).astype(BF16)
            part = lax.dot_general(grads, q_rows, nn, preferred_element_type=F32)
            total = part if total is None else total + part
        out[r] = total.astype(out.dtype)


def attention(which, lengths, q, g, k_prev, k_own, v_prev, v_own, heads, dtype):
    rows = q.shape[0]
    size = heads * 2 * rows * GROUP * rows
    return pl.pallas_call(
        functools.partial(attention_kernel, which, heads),
        in_specs=[pl.BlockSpec(memory_space=pl.ANY)] * 7,
        out_specs=pl.BlockSpec(memory_space=pltpu.VMEM),
        out_shape=jax.ShapeDtypeStruct((heads, 2 * rows, HD), dtype),
        scratch_shapes=[
            pltpu.SMEM(lengths.shape, jnp.int32),
            pltpu.VMEM((heads, rows, GROUP * HD), BF16),
            pltpu.VMEM((heads, rows, GROUP * HD), BF16),
            pltpu.VMEM((heads, 2 * rows, HD), BF16),
            pltpu.VMEM((heads, 2 * rows, HD), BF16),
            pltpu.VMEM((2 * rows, 4 * rows), F32),
            pltpu.SemaphoreType.DMA((6 * heads + 1,)),
        ],
        compiler_params=params(54),
        cost_estimate=cost(6 * size * HD, heads * rows * GROUP * HD * 4, size),
    )(lengths, q, g, k_prev, k_own, v_prev, v_own)


def pack_kernel(sizes, x_ref, *outs):
    ny, nz = sizes
    block = outs[0].shape[2] // CORES
    core, x, y, z_own = position()
    for m, out in enumerate(outs):
        for z in range(nz):
            for c in range(CORES):
                source = (((x ^ (m // ny)) * CORES + c) * nz + z) * ny + (y ^ (m % ny))
                at = pl.ds(pl.multiple_of(source * block, block), block)
                out[z, :, c * block : (c + 1) * block] = x_ref[:, at]


def pack(features, sizes):
    nx, ny, nz = sizes
    rows = features.shape[0]
    shape = jax.ShapeDtypeStruct((nz, rows, DW // (nx * ny * nz)), BF16)
    vmem = pl.BlockSpec(memory_space=pltpu.VMEM)
    return pl.pallas_call(
        functools.partial(pack_kernel, (ny, nz)),
        in_specs=[vmem],
        out_specs=[vmem] * (nx * ny),
        out_shape=[shape] * (nx * ny),
        compiler_params=params(),
        cost_estimate=cost(0, 64 << 20),
    )(features)


def merge_kernel(mine, theirs, out):
    rows = mine.shape[1] // 2
    core = position()[0]

    def write(even, odd):
        for h in range(HALF):
            cols = slice(h * HD, (h + 1) * HD)
            out[:rows, cols] = even[h, :rows]
            out[rows : 2 * rows, cols] = (
                even[h, rows:].astype(F32) + odd[h, :rows].astype(F32)
            ).astype(BF16)
            out[2 * rows :, cols] = odd[h, rows:]

    @pl.when(core == 0)
    def _():
        write(mine, theirs)

    @pl.when(core == 1)
    def _():
        write(theirs, mine)


def merge(mine, theirs):
    rows = mine.shape[1] // 2
    vmem = pl.BlockSpec(memory_space=pltpu.VMEM)
    return pl.pallas_call(
        merge_kernel,
        in_specs=[vmem, vmem],
        out_specs=vmem,
        out_shape=jax.ShapeDtypeStruct((3 * rows, WIDE), BF16),
        compiler_params=params(),
        cost_estimate=cost(rows * WIDE, 7 * rows * WIDE * 2),
    )(mine, theirs)


def weight_kernel(nz, *refs):
    chips, f_same, f_other = refs[:4], refs[4:8], refs[8:12]
    sends, (keep, key_mine, key_theirs, same, other) = refs[12 : 11 + nz], refs[11 + nz :]
    rows = chips[0].shape[0] // 3
    core, x, y, z = position()
    for m in range(4):
        even = chips[m][rows : 2 * rows]
        odd = (chips[m][2 * rows :].astype(F32) + chips[m ^ 2][:rows].astype(F32)).astype(BF16)
        own = jnp.where(core == 0, even, odd)
        far = jnp.where(core == 0, odd, even)
        same[m * rows : (m + 1) * rows] = own
        other[m * rows : (m + 1) * rows] = far
        if m == 0:
            key_mine[...] = own
            key_theirs[...] = far
    tn = (((0,), (0,)), ((), ()))
    for m in (2, 3, 1, 0):
        left = jnp.concatenate([f[z ^ m] for f in f_same], axis=0)
        right = jnp.concatenate([f[z ^ m] for f in f_other], axis=0)
        product = lax.dot_general(same[...], left, tn, preferred_element_type=F32)
        product += lax.dot_general(other[...], right, tn, preferred_element_type=F32)
        if m == 0:
            keep[...] = product
        else:
            sends[m - 1][...] = product.astype(BF16)


def weight(chips, f_same, f_other):
    rows = chips[0].shape[0] // 3
    nz = f_same[0].shape[0]
    vmem = pl.BlockSpec(memory_space=pltpu.VMEM)
    square = (WIDE, f_same[0].shape[2])
    shapes = [jax.ShapeDtypeStruct(square, BF16)] * (nz - 1)
    shapes += [jax.ShapeDtypeStruct(square, F32)] + [jax.ShapeDtypeStruct((rows, WIDE), BF16)] * 2
    return pl.pallas_call(
        functools.partial(weight_kernel, nz),
        in_specs=[vmem] * 12,
        out_specs=[vmem] * len(shapes),
        out_shape=shapes,
        scratch_shapes=[pltpu.VMEM((4 * rows, WIDE), BF16)] * 2,
        compiler_params=params(),
        cost_estimate=cost(2 * 8 * rows * WIDE * 4 * WIDE, 4 << 20),
    )(*chips, *f_same, *f_other)


def reduce_kernel(keep, r1, r2, r3, mine, theirs, squares):
    total = keep[...] + r1[...].astype(F32) + r2[...].astype(F32) + r3[...].astype(F32)
    half = total.shape[1] // 2
    core = position()[0]
    low, high = total[:, :half], total[:, half:]
    mine[...] = jnp.where(core == 0, low, high)
    theirs[...] = jnp.where(core == 0, high, low)
    sums = jnp.sum(low * low + high * high, axis=0, keepdims=True)
    squares[...] = jnp.broadcast_to(sums[None], squares.shape)


def reduce_planes(keep, received, devices):
    cols, both = keep.shape
    vmem = pl.BlockSpec(memory_space=pltpu.VMEM)
    half = jax.ShapeDtypeStruct((cols, both // 2), F32)
    return pl.pallas_call(
        reduce_kernel,
        in_specs=[vmem] * 4,
        out_specs=[vmem] * 3,
        out_shape=[half, half, jax.ShapeDtypeStruct((devices, 1, both // 2), F32)],
        compiler_params=params(),
        cost_estimate=cost(8 * cols * both, cols * both * 14),
    )(keep, *received)


def finish_kernel(squares, mine, theirs, key_mine, key_theirs, key_out, out):
    entries = DW * KVH * HD
    total = jnp.sum(jnp.sum(squares[...], axis=0, keepdims=True), axis=2, keepdims=True)
    root_mean = jnp.sqrt(total / entries + 1e-06)
    factor = jnp.minimum(1.0, 1.0 / root_mean)[0]
    first = position()[0] == 0
    low = (mine[...] * factor).T
    high = (theirs[...] * factor).T
    out[:, :WIDE] = jnp.where(first, low, high)
    out[:, WIDE:] = jnp.where(first, high, low)
    key_out[0, :, :WIDE] = jnp.where(first, key_mine[...], key_theirs[...])
    key_out[0, :, WIDE:] = jnp.where(first, key_theirs[...], key_mine[...])


def finish(squares, mine, theirs, key_mine, key_theirs):
    rows = key_mine.shape[0]
    vmem = pl.BlockSpec(memory_space=pltpu.VMEM)
    return pl.pallas_call(
        finish_kernel,
        in_specs=[vmem] * 5,
        out_specs=[vmem] * 2,
        out_shape=[
            jax.ShapeDtypeStruct((1, rows, KVH * HD), BF16),
            jax.ShapeDtypeStruct((mine.shape[1], KVH * HD), F32),
        ],
        compiler_params=params(),
        cost_estimate=cost(4 * rows * KVH * HD, 4 * rows * KVH * HD * 4),
    )(squares, mine, theirs, key_mine, key_theirs)


def planes(queries, keys, values, grad_out, features, doc_lengths):
    seq_count, dp_count = lax.axis_size("seq"), lax.axis_size("dp")
    devices = seq_count * dp_count
    nx, ny = seq_count // CORES, 2
    nz = dp_count // ny

    def swap(array, mask):
        return lax.ppermute(array, AXES, [(i, i ^ mask) for i in range(devices)])

    core_mask, x_mask, y_mask, z_mask = dp_count, CORES * dp_count, 1, ny
    following = [(i, (i + 1) % seq_count) for i in range(seq_count)]
    k_own, v_own = keys[0], values[0]
    k_prev = lax.ppermute(k_own, "seq", following)
    v_prev = lax.ppermute(v_own, "seq", following)

    masks = [0, y_mask, x_mask, x_mask + y_mask]
    packed = pack(features[0], (nx, ny, nz))
    f_same = [packed[0]] + [swap(part, mask) for part, mask in zip(packed[1:], masks[1:])]

    near = (queries[0], grad_out[0], k_prev, k_own, v_prev, v_own)
    to_send = attention(1, doc_lengths, *near, HALF, BF16)
    theirs = swap(to_send, core_mask)
    mine = attention(0, doc_lengths, *near, HALF, BF16)
    chip = merge(mine, theirs)
    chips = [chip] + [swap(chip, mask) for mask in masks[1:]]
    f_own, _ = lax.optimization_barrier((f_same[0], to_send))
    f_own = swap(f_own, core_mask)
    f_ready, _ = lax.optimization_barrier((f_same[1:], chip))
    f_other = [f_own] + [swap(part, core_mask) for part in f_ready]

    *sends, keep, key_mine, key_send = weight(chips, f_same, f_other)
    received = [swap(sends[m], (m + 1) * z_mask) for m in (1, 2, 0)]
    key_other = swap(key_send, core_mask)
    rows_mine, rows_send, squares = reduce_planes(keep, received, devices)
    rows_other = swap(rows_send, core_mask)
    squares = lax.all_to_all(squares, AXES, 0, 0, tiled=True)
    return finish(squares, rows_mine, rows_other, key_mine, key_other)


def rings(queries, keys, values, grad_out, features, doc_lengths):
    seq_count = lax.axis_size("seq")
    rows = queries.shape[1]
    following = [(i, (i + 1) % seq_count) for i in range(seq_count)]
    preceding = [(i, (i - 1) % seq_count) for i in range(seq_count)]
    k_own, v_own = keys[0], values[0]
    k_prev = lax.ppermute(k_own, "seq", following)
    v_prev = lax.ppermute(v_own, "seq", following)
    near = (queries[0], grad_out[0], k_prev, k_own, v_prev, v_own)
    parts = attention(None, doc_lengths, *near, KVH, F32)
    parts = parts.transpose(1, 0, 2).reshape(2 * rows, KVH * HD)
    after = lax.ppermute(parts[:rows], "seq", preceding)
    key_grad = (parts[rows:] + after).astype(BF16)
    columns = lax.all_to_all(features[0], "seq", split_axis=1, concat_axis=0, tiled=True)
    weight_part = lax.dot_general(
        columns,
        lax.all_gather(key_grad, "seq", axis=0, tiled=True),
        (((0,), (0,)), ((), ())),
        preferred_element_type=F32,
    )
    own_rows = lax.psum_scatter(weight_part, "dp", scatter_dimension=0, tiled=True)
    squares = lax.psum(jnp.sum(own_rows * own_rows), AXES)
    root_mean = jnp.sqrt(squares / (DW * KVH * HD) + 1e-06)
    return (key_grad[None], own_rows * jnp.minimum(1.0, 1.0 / root_mean))


def solution(mesh):
    in_specs = (
        P("dp", "seq", None),
        P("dp", "seq", None),
        P("dp", "seq", None),
        P("dp", "seq", None),
        P("dp", "seq", None),
        P("dp", None),
    )
    out_specs = (P("dp", "seq", None), P(("seq", "dp"), None))
    small = mesh.shape["seq"] == 2 * CORES and mesh.shape["dp"] == 8
    body = planes if small else rings
    return jax.shard_map(body, mesh=mesh, in_specs=in_specs, out_specs=out_specs, check_vma=False)
```

```python
import functools
import math

import jax
import jax.numpy as jnp
from jax import lax
from jax.experimental import pallas as pl
from jax.experimental.pallas import tpu as pltpu
from jax.sharding import PartitionSpec as P

HD = 128
HQ = 32
KVH = 4
DW = 4096
GROUP = HQ // KVH

NEG_FILL = -1e30
AXES = ("seq", "dp")
F32 = jnp.float32
BF16 = jnp.bfloat16
CORES = 2
HALF = KVH // CORES
WIDE = HALF * HD


def params(mib=40):
    return pltpu.CompilerParams(vmem_limit_bytes=mib << 20)


def cost(flops, moved, exps=0):
    return pl.CostEstimate(flops=flops, bytes_accessed=moved, transcendentals=exps)


def position():
    seq, dp = lax.axis_index("seq"), lax.axis_index("dp")
    return seq & 1, seq >> 1, dp & 1, dp >> 1


def attention_kernel(turn, lengths, q, g, k_prev, k_own, v_prev, v_own, *refs):
    outs, scratch = refs[:2], refs[2:]
    ends, q_buf, g_buf, k_buf, v_buf, bias, sems = scratch
    rows = q.shape[0]
    pair = bias.shape[1] // rows
    heads = KVH
    core = position()[0]
    first = (1 - core) * HALF if turn else 0
    waits = [[] for _ in range(heads)]
    length_copy = pltpu.make_async_copy(lengths, ends, sems.at[6 * heads])
    length_copy.start()
    for h in range(heads):
        head = (first + h) & (KVH - 1)
        wide = pl.ds(pl.multiple_of(head * GROUP * HD, GROUP * HD), GROUP * HD)
        one = pl.ds(pl.multiple_of(head * HD, HD), HD)
        moves = [
            (k_prev.at[:, one], k_buf.at[h, :rows]),
            (k_own.at[:, one], k_buf.at[h, rows:]),
            (q.at[:, wide], q_buf.at[h]),
            (v_prev.at[:, one], v_buf.at[h, :rows]),
            (v_own.at[:, one], v_buf.at[h, rows:]),
            (g.at[:, wide], g_buf.at[h]),
        ]
        for n, (source, target) in enumerate(moves):
            copy = pltpu.make_async_copy(source, target, sems.at[6 * h + n])
            copy.start()
            waits[h].append(copy)
    length_copy.wait()
    base = lax.axis_index("seq") * rows
    query_pos = base + lax.broadcasted_iota(jnp.int32, (1, rows), 1)
    start = jnp.zeros((1, rows), jnp.int32)
    end = jnp.int32(0)
    for d in range(ends.shape[1]):
        end = end + ends[0, d]
        start = jnp.where(end <= query_pos, end, start)
    key_pos = base - rows + lax.broadcasted_iota(jnp.int32, (2 * rows, rows), 0)
    visible = (key_pos >= start) & (key_pos <= query_pos)
    hidden = jnp.where(visible, 0.0, NEG_FILL).astype(F32)
    for n in range(pair):
        bias[:, n * rows : (n + 1) * rows] = hidden

    scale = 1.0 / math.sqrt(HD)
    scale2 = scale * math.log2(math.e)
    nt = (((1,), (1,)), ((), ()))
    nn = (((1,), (0,)), ((), ()))
    for r in range(heads):
        for copy in waits[r]:
            copy.wait()
        key, value = k_buf[r], v_buf[r]
        total = None
        for h in range(0, GROUP, pair):
            cols = [slice((h + n) * HD, (h + n + 1) * HD) for n in range(pair)]
            q_rows = jnp.concatenate([q_buf[r, :, c] for c in cols], axis=0)
            g_rows = jnp.concatenate([g_buf[r, :, c] for c in cols], axis=0)
            scores = lax.dot_general(key, q_rows, nt, preferred_element_type=F32)
            weights = lax.dot_general(value, g_rows, nt, preferred_element_type=F32)
            scores = scores * scale2 + bias[...]
            exponent = jnp.exp2(scores - jnp.max(scores, axis=0, keepdims=True))
            inverse = 1.0 / jnp.sum(exponent, axis=0, keepdims=True)
            delta = jnp.sum(exponent * weights, axis=0, keepdims=True) * inverse
            grads = ((exponent * (inverse * scale)) * (weights - delta)).astype(BF16)
            part = lax.dot_general(grads, q_rows, nn, preferred_element_type=F32)
            total = part if total is None else total + part
        outs[r // HALF][r % HALF] = total.astype(outs[0].dtype)


def attention(turn, lengths, q, g, k_prev, k_own, v_prev, v_own, dtype):
    rows = q.shape[0]
    heads = KVH
    size = heads * 2 * rows * GROUP * rows
    return pl.pallas_call(
        functools.partial(attention_kernel, turn),
        in_specs=[pl.BlockSpec(memory_space=pl.ANY)] * 7,
        out_specs=[pl.BlockSpec(memory_space=pltpu.VMEM)] * 2,
        out_shape=[jax.ShapeDtypeStruct((HALF, 2 * rows, HD), dtype)] * 2,
        scratch_shapes=[
            pltpu.SMEM(lengths.shape, jnp.int32),
            pltpu.VMEM((heads, rows, GROUP * HD), BF16),
            pltpu.VMEM((heads, rows, GROUP * HD), BF16),
            pltpu.VMEM((heads, 2 * rows, HD), BF16),
            pltpu.VMEM((heads, 2 * rows, HD), BF16),
            pltpu.VMEM((2 * rows, 4 * rows), F32),
            pltpu.SemaphoreType.DMA((6 * heads + 1,)),
        ],
        compiler_params=params(54),
        cost_estimate=cost(6 * size * HD, heads * rows * GROUP * HD * 4, size),
    )(lengths, q, g, k_prev, k_own, v_prev, v_own)


def pack_kernel(sizes, x_ref, *outs):
    ny, nz = sizes
    block = outs[0].shape[2] // CORES
    core, x, y, z_own = position()
    for m, out in enumerate(outs):
        for z in range(nz):
            for c in range(CORES):
                source = (((x ^ (m // ny)) * CORES + c) * nz + z) * ny + (y ^ (m % ny))
                at = pl.ds(pl.multiple_of(source * block, block), block)
                out[z, :, c * block : (c + 1) * block] = x_ref[:, at]


def pack(features, sizes):
    nx, ny, nz = sizes
    rows = features.shape[0]
    shape = jax.ShapeDtypeStruct((nz, rows, DW // (nx * ny * nz)), BF16)
    vmem = pl.BlockSpec(memory_space=pltpu.VMEM)
    return pl.pallas_call(
        functools.partial(pack_kernel, (ny, nz)),
        in_specs=[vmem],
        out_specs=[vmem] * (nx * ny),
        out_shape=[shape] * (nx * ny),
        compiler_params=params(),
        cost_estimate=cost(0, 64 << 20),
    )(features)


def merge_kernel(mine, theirs, *outs):
    rows = mine.shape[1] // 2
    core = position()[0]

    def write(even, odd):
        for h in range(HALF):
            out = outs[h]
            out[:rows] = even[h, :rows]
            total = even[h, rows:].astype(F32) + odd[h, :rows].astype(F32)
            out[rows : 2 * rows] = total.astype(BF16)
            out[2 * rows :] = odd[h, rows:]

    @pl.when(core == 0)
    def _():
        write(mine, theirs)

    @pl.when(core == 1)
    def _():
        write(theirs, mine)


def merge(mine, theirs):
    rows = mine.shape[1] // 2
    vmem = pl.BlockSpec(memory_space=pltpu.VMEM)
    return pl.pallas_call(
        merge_kernel,
        in_specs=[vmem, vmem],
        out_specs=[vmem] * HALF,
        out_shape=[jax.ShapeDtypeStruct((3 * rows, HD), BF16)] * HALF,
        compiler_params=params(),
        cost_estimate=cost(rows * WIDE, 7 * rows * WIDE * 2),
    )(mine, theirs)


def weight_kernel(nz, *refs):
    chips = (refs[0], refs[1], refs[2], refs[3])
    f_same = (refs[4], refs[5], refs[6], refs[7])
    f_other = [refs[8].at[m] for m in range(4)]
    sends, (keep, key_mine, key_theirs, same, other) = refs[9 : 8 + nz], refs[8 + nz :]
    rows = chips[0].shape[0] // 3
    core, x, y, z = position()
    for m in range(4):
        even = chips[m][rows : 2 * rows]
        odd = (chips[m][2 * rows :].astype(F32) + chips[m ^ 2][:rows].astype(F32)).astype(BF16)
        own = jnp.where(core == 0, even, odd)
        far = jnp.where(core == 0, odd, even)
        same[m * rows : (m + 1) * rows] = own
        other[m * rows : (m + 1) * rows] = far
        if m == 0:
            key_mine[...] = own
            key_theirs[...] = far
    tn = (((0,), (0,)), ((), ()))
    for m in (2, 3, 1, 0):
        left = jnp.concatenate([f[z ^ m] for f in f_same], axis=0)
        right = jnp.concatenate([f[z ^ m] for f in f_other], axis=0)
        product = lax.dot_general(same[...], left, tn, preferred_element_type=F32)
        product += lax.dot_general(other[...], right, tn, preferred_element_type=F32)
        if m == 0:
            keep[...] = product
        else:
            sends[m - 1][...] = product.astype(BF16)


def weight(chips, f_same, f_other):
    rows = chips[0].shape[0] // 3
    nz = f_same[0].shape[0]
    vmem = pl.BlockSpec(memory_space=pltpu.VMEM)
    square = (HD, f_same[0].shape[2])
    shapes = [jax.ShapeDtypeStruct(square, BF16)] * (nz - 1)
    shapes += [jax.ShapeDtypeStruct(square, F32)] + [jax.ShapeDtypeStruct((rows, HD), BF16)] * 2
    return pl.pallas_call(
        functools.partial(weight_kernel, nz),
        in_specs=[vmem] * 9,
        out_specs=[vmem] * len(shapes),
        out_shape=shapes,
        scratch_shapes=[pltpu.VMEM((4 * rows, HD), BF16)] * 2,
        compiler_params=params(),
        cost_estimate=cost(2 * 8 * rows * HD * 4 * WIDE, 4 << 20),
    )(*[chips[m] for m in (0, 1, 2, 3)], *[f_same[m] for m in (0, 1, 2, 3)], *f_other)


def squares_kernel(*refs):
    squares = refs[-1]
    sums = 0.0
    for h in range(HALF):
        keep, r1, r2, r3 = refs[4 * h : 4 * h + 4]
        total = keep[...] + r1[...].astype(F32) + r2[...].astype(F32) + r3[...].astype(F32)
        half = total.shape[1] // 2
        low, high = total[:, :half], total[:, half:]
        sums += jnp.sum(low * low + high * high, axis=0, keepdims=True)
    squares[...] = jnp.broadcast_to(sums[None], squares.shape)


def plane_squares(parts, devices):
    cols, both = parts[0].shape
    vmem = pl.BlockSpec(memory_space=pltpu.VMEM)
    return pl.pallas_call(
        squares_kernel,
        in_specs=[vmem] * len(parts),
        out_specs=vmem,
        out_shape=jax.ShapeDtypeStruct((devices, 1, both // 2), F32),
        compiler_params=params(),
        cost_estimate=cost(16 * cols * both, cols * both * 20),
    )(*parts)


def rows_kernel(*refs):
    mine, theirs = refs[-2:]
    core = position()[0]
    for h in range(HALF):
        keep, r1, r2, r3 = refs[4 * h : 4 * h + 4]
        total = keep[...] + r1[...].astype(F32) + r2[...].astype(F32) + r3[...].astype(F32)
        half = total.shape[1] // 2
        low, high = total[:, :half].T, total[:, half:].T
        cols = slice(h * HD, (h + 1) * HD)
        mine[:, cols] = jnp.where(core == 0, low, high)
        theirs[:, cols] = jnp.where(core == 0, high, low)


def plane_rows(parts):
    cols, both = parts[0].shape
    vmem = pl.BlockSpec(memory_space=pltpu.VMEM)
    return pl.pallas_call(
        rows_kernel,
        in_specs=[vmem] * len(parts),
        out_specs=[vmem] * 2,
        out_shape=[jax.ShapeDtypeStruct((both // 2, WIDE), F32)] * 2,
        compiler_params=params(),
        cost_estimate=cost(16 * cols * both, cols * both * 28),
    )(*parts)


def join_kernel(mine, theirs, *refs):
    keys_mine, keys_theirs, (out, key_out) = refs[:HALF], refs[HALF : 2 * HALF], refs[2 * HALF :]
    first = position()[0] == 0
    out[:, :WIDE] = jnp.where(first, mine[...], theirs[...])
    out[:, WIDE:] = jnp.where(first, theirs[...], mine[...])
    for h in range(HALF):
        own, far = keys_mine[h][...], keys_theirs[h][...]
        key_out[0, :, h * HD : (h + 1) * HD] = jnp.where(first, own, far)
        key_out[0, :, WIDE + h * HD : WIDE + (h + 1) * HD] = jnp.where(first, far, own)


def join(mine, theirs, keys_mine, keys_theirs):
    rows = keys_mine[0].shape[0]
    vmem = pl.BlockSpec(memory_space=pltpu.VMEM)
    return pl.pallas_call(
        join_kernel,
        in_specs=[vmem] * (2 + 2 * HALF),
        out_specs=[vmem] * 2,
        out_shape=[
            jax.ShapeDtypeStruct((mine.shape[0], KVH * HD), F32),
            jax.ShapeDtypeStruct((1, rows, KVH * HD), BF16),
        ],
        compiler_params=params(),
        cost_estimate=cost(0, 12 * rows * KVH * HD),
    )(mine, theirs, *keys_mine, *keys_theirs)


def clip_kernel(squares, rows, out):
    entries = DW * KVH * HD
    total = jnp.sum(jnp.sum(squares[...], axis=0, keepdims=True), axis=2, keepdims=True)
    root_mean = jnp.sqrt(total / entries + 1e-06)
    out[...] = rows[...] * jnp.minimum(1.0, 1.0 / root_mean)[0]


def clip(squares, rows):
    vmem = pl.BlockSpec(memory_space=pltpu.VMEM)
    return pl.pallas_call(
        clip_kernel,
        in_specs=[vmem] * 2,
        out_specs=vmem,
        out_shape=jax.ShapeDtypeStruct(rows.shape, F32),
        compiler_params=params(),
        cost_estimate=cost(rows.size, 8 * rows.size),
    )(squares, rows)


def planes(queries, keys, values, grad_out, features, doc_lengths):
    seq_count, dp_count = lax.axis_size("seq"), lax.axis_size("dp")
    devices = seq_count * dp_count
    nx, ny = seq_count // CORES, 2
    nz = dp_count // ny

    def swap(array, mask):
        return lax.ppermute(array, AXES, [(i, i ^ mask) for i in range(devices)])

    core_mask, x_mask, y_mask, z_mask = dp_count, CORES * dp_count, 1, ny
    following = [(i, (i + 1) % seq_count) for i in range(seq_count)]
    k_own, v_own = keys[0], values[0]
    k_prev = lax.ppermute(k_own, "seq", following)
    v_prev = lax.ppermute(v_own, "seq", following)

    masks = [0, y_mask, x_mask, x_mask + y_mask]
    packed = pack(features[0], (nx, ny, nz))
    f_same = [packed[0]] + [swap(part, mask) for part, mask in zip(packed[1:], masks[1:])]

    near = (queries[0], grad_out[0], k_prev, k_own, v_prev, v_own)
    to_send, mine = attention(True, doc_lengths, *near, BF16)
    theirs = swap(to_send, core_mask)
    pieces = merge(mine, theirs)
    chips = [[piece] + [swap(piece, mask) for mask in masks[1:]] for piece in pieces]
    f_ready, _ = lax.optimization_barrier((f_same, pieces[0]))
    far = swap(jnp.stack(f_ready), core_mask)
    f_other = [far]

    parts, keys_mine, keys_other = [], [], []
    for h in range(HALF):
        *sends, keep, key_mine, key_send = weight(chips[h], f_same, f_other)
        parts += [keep] + [swap(sends[m], (m + 1) * z_mask) for m in (1, 2, 0)]
        keys_mine.append(key_mine)
        keys_other.append(swap(key_send, core_mask))
    squares = plane_squares(parts, devices)
    parts[0], squares = lax.optimization_barrier((parts[0], squares))
    squares = lax.all_to_all(squares, AXES, 0, 0, tiled=True)
    rows_mine, rows_send = plane_rows(parts)
    rows_other = swap(rows_send, core_mask)
    rows, key_grad = join(rows_mine, rows_other, keys_mine, keys_other)
    return key_grad, clip(squares, rows)


def rings(queries, keys, values, grad_out, features, doc_lengths):
    seq_count = lax.axis_size("seq")
    rows = queries.shape[1]
    following = [(i, (i + 1) % seq_count) for i in range(seq_count)]
    preceding = [(i, (i - 1) % seq_count) for i in range(seq_count)]
    k_own, v_own = keys[0], values[0]
    k_prev = lax.ppermute(k_own, "seq", following)
    v_prev = lax.ppermute(v_own, "seq", following)
    near = (queries[0], grad_out[0], k_prev, k_own, v_prev, v_own)
    parts = jnp.concatenate(attention(False, doc_lengths, *near, F32), axis=0)
    parts = parts.transpose(1, 0, 2).reshape(2 * rows, KVH * HD)
    after = lax.ppermute(parts[:rows], "seq", preceding)
    key_grad = (parts[rows:] + after).astype(BF16)
    columns = lax.all_to_all(features[0], "seq", split_axis=1, concat_axis=0, tiled=True)
    weight_part = lax.dot_general(
        columns,
        lax.all_gather(key_grad, "seq", axis=0, tiled=True),
        (((0,), (0,)), ((), ())),
        preferred_element_type=F32,
    )
    own_rows = lax.psum_scatter(weight_part, "dp", scatter_dimension=0, tiled=True)
    squares = lax.psum(jnp.sum(own_rows * own_rows), AXES)
    root_mean = jnp.sqrt(squares / (DW * KVH * HD) + 1e-06)
    return (key_grad[None], own_rows * jnp.minimum(1.0, 1.0 / root_mean))


def solution(mesh):
    in_specs = (
        P("dp", "seq", None),
        P("dp", "seq", None),
        P("dp", "seq", None),
        P("dp", "seq", None),
        P("dp", "seq", None),
        P("dp", None),
    )
    out_specs = (P("dp", "seq", None), P(("seq", "dp"), None))
    small = mesh.shape["seq"] == 2 * CORES and mesh.shape["dp"] == 8
    body = planes if small else rings
    return jax.shard_map(body, mesh=mesh, in_specs=in_specs, out_specs=out_specs, check_vma=False)
```

```python
import functools
import math

import jax
import jax.numpy as jnp
from jax import lax
from jax.experimental import pallas as pl
from jax.experimental.pallas import tpu as pltpu
from jax.sharding import PartitionSpec as P

HD = 128
HQ = 32
KVH = 4
DW = 4096
GROUP = HQ // KVH

NEG_FILL = -1e30
AXES = ("seq", "dp")
F32 = jnp.float32
BF16 = jnp.bfloat16
CORES = 2
HALF = KVH // CORES
WIDE = HALF * HD


def params(mib=40):
    return pltpu.CompilerParams(vmem_limit_bytes=mib << 20)


def cost(flops, moved, exps=0):
    return pl.CostEstimate(flops=flops, bytes_accessed=moved, transcendentals=exps)


def position():
    seq, dp = lax.axis_index("seq"), lax.axis_index("dp")
    return seq & 1, seq >> 1, dp & 1, dp >> 1


def attention_kernel(turn, lengths, q, g, k_prev, k_own, v_prev, v_own, *refs):
    outs, scratch = refs[:2], refs[2:]
    ends, q_buf, g_buf, k_buf, v_buf, bias, sems = scratch
    rows = q.shape[0]
    pair = bias.shape[1] // rows
    heads = KVH
    core = position()[0]
    first = (1 - core) * HALF if turn else 0
    waits = [[] for _ in range(heads)]
    length_copy = pltpu.make_async_copy(lengths, ends, sems.at[6 * heads])
    length_copy.start()
    for h in range(heads):
        head = (first + h) & (KVH - 1)
        wide = pl.ds(pl.multiple_of(head * GROUP * HD, GROUP * HD), GROUP * HD)
        one = pl.ds(pl.multiple_of(head * HD, HD), HD)
        moves = [
            (k_prev.at[:, one], k_buf.at[h, :rows]),
            (k_own.at[:, one], k_buf.at[h, rows:]),
            (q.at[:, wide], q_buf.at[h]),
            (v_prev.at[:, one], v_buf.at[h, :rows]),
            (v_own.at[:, one], v_buf.at[h, rows:]),
            (g.at[:, wide], g_buf.at[h]),
        ]
        for n, (source, target) in enumerate(moves):
            copy = pltpu.make_async_copy(source, target, sems.at[6 * h + n])
            copy.start()
            waits[h].append(copy)
    length_copy.wait()
    base = lax.axis_index("seq") * rows
    query_pos = base + lax.broadcasted_iota(jnp.int32, (1, rows), 1)
    start = jnp.zeros((1, rows), jnp.int32)
    end = jnp.int32(0)
    for d in range(ends.shape[1]):
        end = end + ends[0, d]
        start = jnp.where(end <= query_pos, end, start)
    key_pos = base - rows + lax.broadcasted_iota(jnp.int32, (2 * rows, rows), 0)
    visible = (key_pos >= start) & (key_pos <= query_pos)
    hidden = jnp.where(visible, 0.0, NEG_FILL).astype(F32)
    for n in range(pair):
        bias[:, n * rows : (n + 1) * rows] = hidden

    scale = 1.0 / math.sqrt(HD)
    scale2 = scale * math.log2(math.e)
    nt = (((1,), (1,)), ((), ()))
    nn = (((1,), (0,)), ((), ()))
    for r in range(heads):
        for copy in waits[r]:
            copy.wait()
        key, value = k_buf[r], v_buf[r]
        total = None
        for h in range(0, GROUP, pair):
            cols = [slice((h + n) * HD, (h + n + 1) * HD) for n in range(pair)]
            q_rows = jnp.concatenate([q_buf[r, :, c] for c in cols], axis=0)
            g_rows = jnp.concatenate([g_buf[r, :, c] for c in cols], axis=0)
            scores = lax.dot_general(key, q_rows, nt, preferred_element_type=F32)
            weights = lax.dot_general(value, g_rows, nt, preferred_element_type=F32)
            scores = scores * scale2 + bias[...]
            exponent = jnp.exp2(scores - jnp.max(scores, axis=0, keepdims=True))
            inverse = 1.0 / jnp.sum(exponent, axis=0, keepdims=True)
            delta = jnp.sum(exponent * weights, axis=0, keepdims=True) * inverse
            grads = ((exponent * (inverse * scale)) * (weights - delta)).astype(BF16)
            part = lax.dot_general(grads, q_rows, nn, preferred_element_type=F32)
            total = part if total is None else total + part
        outs[r // HALF][r % HALF] = total.astype(outs[0].dtype)


def attention(turn, lengths, q, g, k_prev, k_own, v_prev, v_own, dtype):
    rows = q.shape[0]
    heads = KVH
    size = heads * 2 * rows * GROUP * rows
    return pl.pallas_call(
        functools.partial(attention_kernel, turn),
        in_specs=[pl.BlockSpec(memory_space=pl.ANY)] * 7,
        out_specs=[pl.BlockSpec(memory_space=pltpu.VMEM)] * 2,
        out_shape=[jax.ShapeDtypeStruct((HALF, 2 * rows, HD), dtype)] * 2,
        scratch_shapes=[
            pltpu.SMEM(lengths.shape, jnp.int32),
            pltpu.VMEM((heads, rows, GROUP * HD), BF16),
            pltpu.VMEM((heads, rows, GROUP * HD), BF16),
            pltpu.VMEM((heads, 2 * rows, HD), BF16),
            pltpu.VMEM((heads, 2 * rows, HD), BF16),
            pltpu.VMEM((2 * rows, 4 * rows), F32),
            pltpu.SemaphoreType.DMA((6 * heads + 1,)),
        ],
        compiler_params=params(54),
        cost_estimate=cost(6 * size * HD, heads * rows * GROUP * HD * 4, size),
    )(lengths, q, g, k_prev, k_own, v_prev, v_own)


def pack_kernel(sizes, x_ref, *outs):
    ny, nz = sizes
    block = outs[0].shape[2] // CORES
    core, x, y, z_own = position()
    for m, out in enumerate(outs):
        for z in range(nz):
            for c in range(CORES):
                source = (((x ^ (m // ny)) * CORES + c) * nz + z) * ny + (y ^ (m % ny))
                at = pl.ds(pl.multiple_of(source * block, block), block)
                out[z, :, c * block : (c + 1) * block] = x_ref[:, at]


def pack(features, sizes):
    nx, ny, nz = sizes
    rows = features.shape[0]
    shape = jax.ShapeDtypeStruct((nz, rows, DW // (nx * ny * nz)), BF16)
    vmem = pl.BlockSpec(memory_space=pltpu.VMEM)
    return pl.pallas_call(
        functools.partial(pack_kernel, (ny, nz)),
        in_specs=[vmem],
        out_specs=[vmem] * (nx * ny),
        out_shape=[shape] * (nx * ny),
        compiler_params=params(),
        cost_estimate=cost(0, 64 << 20),
    )(features)


def merge_kernel(mine, theirs, *outs):
    rows = mine.shape[1] // 2
    core = position()[0]

    def write(even, odd):
        for h in range(HALF):
            out = outs[h]
            out[:rows] = even[h, :rows]
            total = even[h, rows:].astype(F32) + odd[h, :rows].astype(F32)
            out[rows : 2 * rows] = total.astype(BF16)
            out[2 * rows :] = odd[h, rows:]

    @pl.when(core == 0)
    def _():
        write(mine, theirs)

    @pl.when(core == 1)
    def _():
        write(theirs, mine)


def merge(mine, theirs):
    rows = mine.shape[1] // 2
    vmem = pl.BlockSpec(memory_space=pltpu.VMEM)
    return pl.pallas_call(
        merge_kernel,
        in_specs=[vmem, vmem],
        out_specs=[vmem] * HALF,
        out_shape=[jax.ShapeDtypeStruct((3 * rows, HD), BF16)] * HALF,
        compiler_params=params(),
        cost_estimate=cost(rows * WIDE, 7 * rows * WIDE * 2),
    )(mine, theirs)


def weight_kernel(nz, *refs):
    chips = (refs[0], refs[1], refs[2], refs[3])
    f_same = (refs[4], refs[5], refs[6], refs[7])
    f_other = [refs[8].at[m] for m in range(4)]
    sends, (keep, key_mine, key_theirs, same, other) = refs[9 : 8 + nz], refs[8 + nz :]
    rows = chips[0].shape[0] // 3
    core, x, y, z = position()
    for m in range(4):
        even = chips[m][rows : 2 * rows]
        odd = (chips[m][2 * rows :].astype(F32) + chips[m ^ 2][:rows].astype(F32)).astype(BF16)
        own = jnp.where(core == 0, even, odd)
        far = jnp.where(core == 0, odd, even)
        same[m * rows : (m + 1) * rows] = own
        other[m * rows : (m + 1) * rows] = far
        if m == 0:
            key_mine[...] = own
            key_theirs[...] = far
    tn = (((0,), (0,)), ((), ()))
    for m in (2, 3, 1, 0):
        left = jnp.concatenate([f[z ^ m] for f in f_same], axis=0)
        right = jnp.concatenate([f[z ^ m] for f in f_other], axis=0)
        product = lax.dot_general(same[...], left, tn, preferred_element_type=F32)
        product += lax.dot_general(other[...], right, tn, preferred_element_type=F32)
        if m == 0:
            keep[...] = product
        else:
            sends[m - 1][...] = product.astype(BF16)


def weight(chips, f_same, f_other):
    rows = chips[0].shape[0] // 3
    nz = f_same[0].shape[0]
    vmem = pl.BlockSpec(memory_space=pltpu.VMEM)
    square = (HD, f_same[0].shape[2])
    shapes = [jax.ShapeDtypeStruct(square, BF16)] * (nz - 1)
    shapes += [jax.ShapeDtypeStruct(square, F32)] + [jax.ShapeDtypeStruct((rows, HD), BF16)] * 2
    return pl.pallas_call(
        functools.partial(weight_kernel, nz),
        in_specs=[vmem] * 9,
        out_specs=[vmem] * len(shapes),
        out_shape=shapes,
        scratch_shapes=[pltpu.VMEM((4 * rows, HD), BF16)] * 2,
        compiler_params=params(),
        cost_estimate=cost(2 * 8 * rows * HD * 4 * WIDE, 4 << 20),
    )(*[chips[m] for m in (0, 1, 2, 3)], *[f_same[m] for m in (0, 1, 2, 3)], *f_other)


def squares_kernel(*refs):
    squares = refs[-1]
    sums = 0.0
    for h in range(HALF):
        keep, r1, r2, r3 = refs[4 * h : 4 * h + 4]
        total = keep[...] + r1[...].astype(F32) + r2[...].astype(F32) + r3[...].astype(F32)
        half = total.shape[1] // 2
        low, high = total[:, :half], total[:, half:]
        sums += jnp.sum(low * low + high * high, axis=0, keepdims=True)
    squares[...] = jnp.broadcast_to(sums[None], squares.shape)


def plane_squares(parts, devices):
    cols, both = parts[0].shape
    vmem = pl.BlockSpec(memory_space=pltpu.VMEM)
    return pl.pallas_call(
        squares_kernel,
        in_specs=[vmem] * len(parts),
        out_specs=vmem,
        out_shape=jax.ShapeDtypeStruct((devices, 1, both // 2), F32),
        compiler_params=params(),
        cost_estimate=cost(16 * cols * both, cols * both * 20),
    )(*parts)


def rows_kernel(*refs):
    keys, (mine, theirs) = refs[4 * HALF : 5 * HALF], refs[-2:]
    core = position()[0]
    for h in range(HALF):
        keep, r1, r2, r3 = refs[4 * h : 4 * h + 4]
        total = keep[...] + r1[...].astype(F32) + r2[...].astype(F32) + r3[...].astype(F32)
        half = total.shape[1] // 2
        low, high = total[:, :half].T, total[:, half:].T
        cols = slice(h * HD, (h + 1) * HD)
        mine[:, cols] = jnp.where(core == 0, low, high)
        theirs[:, cols] = jnp.where(core == 0, high, low)
        theirs[:, WIDE + h * HD : WIDE + (h + 1) * HD] = keys[h][...].astype(F32)


def plane_rows(parts, keys):
    cols, both = parts[0].shape
    vmem = pl.BlockSpec(memory_space=pltpu.VMEM)
    return pl.pallas_call(
        rows_kernel,
        in_specs=[vmem] * (len(parts) + len(keys)),
        out_specs=[vmem] * 2,
        out_shape=[jax.ShapeDtypeStruct((both // 2, n * WIDE), F32) for n in (1, 2)],
        compiler_params=params(),
        cost_estimate=cost(16 * cols * both, cols * both * 28),
    )(*parts, *keys)


def join_kernel(mine, theirs, *refs):
    keys, (out, key_out) = refs[:HALF], refs[HALF:]
    first = position()[0] == 0
    rows, far = theirs[:, :WIDE], theirs[:, WIDE:].astype(BF16)
    key = jnp.concatenate([k[...] for k in keys], axis=1)
    out[:, :WIDE] = jnp.where(first, mine[...], rows)
    out[:, WIDE:] = jnp.where(first, rows, mine[...])
    key_out[0, :, :WIDE] = jnp.where(first, key, far)
    key_out[0, :, WIDE:] = jnp.where(first, far, key)


def join(mine, theirs, keys):
    rows = keys[0].shape[0]
    vmem = pl.BlockSpec(memory_space=pltpu.VMEM)
    return pl.pallas_call(
        join_kernel,
        in_specs=[vmem] * (2 + HALF),
        out_specs=[vmem] * 2,
        out_shape=[
            jax.ShapeDtypeStruct((mine.shape[0], KVH * HD), F32),
            jax.ShapeDtypeStruct((1, rows, KVH * HD), BF16),
        ],
        compiler_params=params(),
        cost_estimate=cost(0, 12 * rows * KVH * HD),
    )(mine, theirs, *keys)


def clip_kernel(squares, rows, out):
    entries = DW * KVH * HD
    total = jnp.sum(jnp.sum(squares[...], axis=0, keepdims=True), axis=2, keepdims=True)
    root_mean = jnp.sqrt(total / entries + 1e-06)
    out[...] = rows[...] * jnp.minimum(1.0, 1.0 / root_mean)[0]


def clip(squares, rows):
    vmem = pl.BlockSpec(memory_space=pltpu.VMEM)
    return pl.pallas_call(
        clip_kernel,
        in_specs=[vmem] * 2,
        out_specs=vmem,
        out_shape=jax.ShapeDtypeStruct(rows.shape, F32),
        compiler_params=params(),
        cost_estimate=cost(rows.size, 8 * rows.size),
    )(squares, rows)


def planes(queries, keys, values, grad_out, features, doc_lengths):
    seq_count, dp_count = lax.axis_size("seq"), lax.axis_size("dp")
    devices = seq_count * dp_count
    nx, ny = seq_count // CORES, 2
    nz = dp_count // ny

    def swap(array, mask):
        return lax.ppermute(array, AXES, [(i, i ^ mask) for i in range(devices)])

    core_mask, x_mask, y_mask, z_mask = dp_count, CORES * dp_count, 1, ny
    following = [(i, (i + 1) % seq_count) for i in range(seq_count)]
    k_own, v_own = keys[0], values[0]
    k_prev = lax.ppermute(k_own, "seq", following)
    v_prev = lax.ppermute(v_own, "seq", following)

    masks = [0, y_mask, x_mask, x_mask + y_mask]
    packed = pack(features[0], (nx, ny, nz))
    f_same = [packed[0]] + [swap(part, mask) for part, mask in zip(packed[1:], masks[1:])]

    near = (queries[0], grad_out[0], k_prev, k_own, v_prev, v_own)
    to_send, mine = attention(True, doc_lengths, *near, BF16)
    theirs = swap(to_send, core_mask)
    pieces = merge(mine, theirs)
    f_ready, _ = lax.optimization_barrier((f_same, pieces[0]))
    far, late = lax.optimization_barrier((swap(jnp.stack(f_ready), core_mask), pieces[1]))
    f_other = [far]
    chips = [[piece] + [swap(piece, mask) for mask in masks[1:]] for piece in (pieces[0], late)]

    parts, keys_mine, keys_send = [], [], []
    for h in range(HALF):
        *sends, keep, key_mine, key_send = weight(chips[h], f_same, f_other)
        parts += [keep] + [swap(sends[m], (m + 1) * z_mask) for m in (1, 2, 0)]
        keys_mine.append(key_mine)
        keys_send.append(key_send)
    squares = plane_squares(parts, devices)
    parts[0], squares = lax.optimization_barrier((parts[0], squares))
    squares = lax.all_to_all(squares, AXES, 0, 0, tiled=True)
    rows_mine, rows_send = plane_rows(parts, keys_send)
    rows_other = swap(rows_send, core_mask)
    rows, key_grad = join(rows_mine, rows_other, keys_mine)
    return key_grad, clip(squares, rows)


def rings(queries, keys, values, grad_out, features, doc_lengths):
    seq_count = lax.axis_size("seq")
    rows = queries.shape[1]
    following = [(i, (i + 1) % seq_count) for i in range(seq_count)]
    preceding = [(i, (i - 1) % seq_count) for i in range(seq_count)]
    k_own, v_own = keys[0], values[0]
    k_prev = lax.ppermute(k_own, "seq", following)
    v_prev = lax.ppermute(v_own, "seq", following)
    near = (queries[0], grad_out[0], k_prev, k_own, v_prev, v_own)
    parts = jnp.concatenate(attention(False, doc_lengths, *near, F32), axis=0)
    parts = parts.transpose(1, 0, 2).reshape(2 * rows, KVH * HD)
    after = lax.ppermute(parts[:rows], "seq", preceding)
    key_grad = (parts[rows:] + after).astype(BF16)
    columns = lax.all_to_all(features[0], "seq", split_axis=1, concat_axis=0, tiled=True)
    weight_part = lax.dot_general(
        columns,
        lax.all_gather(key_grad, "seq", axis=0, tiled=True),
        (((0,), (0,)), ((), ())),
        preferred_element_type=F32,
    )
    own_rows = lax.psum_scatter(weight_part, "dp", scatter_dimension=0, tiled=True)
    squares = lax.psum(jnp.sum(own_rows * own_rows), AXES)
    root_mean = jnp.sqrt(squares / (DW * KVH * HD) + 1e-06)
    return (key_grad[None], own_rows * jnp.minimum(1.0, 1.0 / root_mean))


def solution(mesh):
    in_specs = (
        P("dp", "seq", None),
        P("dp", "seq", None),
        P("dp", "seq", None),
        P("dp", "seq", None),
        P("dp", "seq", None),
        P("dp", None),
    )
    out_specs = (P("dp", "seq", None), P(("seq", "dp"), None))
    small = mesh.shape["seq"] == 2 * CORES and mesh.shape["dp"] == 8
    body = planes if small else rings
    return jax.shard_map(body, mesh=mesh, in_specs=in_specs, out_specs=out_specs, check_vma=False)
```

```python
import functools
import math

import jax
import jax.numpy as jnp
from jax import lax
from jax.experimental import pallas as pl
from jax.experimental.pallas import tpu as pltpu
from jax.sharding import PartitionSpec as P

HD = 128
HQ = 32
KVH = 4
DW = 4096
GROUP = HQ // KVH

NEG_FILL = -1e30
AXES = ("seq", "dp")
F32 = jnp.float32
BF16 = jnp.bfloat16
CORES = 2
ORDER = ((0, 2, 1, 3), (0, 2, 1, 3))
SUMS = ((1, 2, 0), (1, 2, 0))
HALF = KVH // CORES
WIDE = HALF * HD


def params(mib=40):
    return pltpu.CompilerParams(vmem_limit_bytes=mib << 20)


def cost(flops, moved, exps=0):
    return pl.CostEstimate(flops=flops, bytes_accessed=moved, transcendentals=exps)


def position():
    seq, dp = lax.axis_index("seq"), lax.axis_index("dp")
    return seq & 1, seq >> 1, dp & 1, dp >> 1


def attention_kernel(turn, lengths, q, g, k_prev, k_own, v_prev, v_own, *refs):
    outs, scratch = refs[:2], refs[2:]
    ends, q_buf, g_buf, k_buf, v_buf, bias, sems = scratch
    rows = q.shape[0]
    pair = bias.shape[1] // rows
    heads = KVH
    core = position()[0]
    first = (1 - core) * HALF if turn else 0
    waits = [[] for _ in range(heads)]
    length_copy = pltpu.make_async_copy(lengths, ends, sems.at[6 * heads])
    length_copy.start()
    for h in range(heads):
        head = (first + h) & (KVH - 1)
        wide = pl.ds(pl.multiple_of(head * GROUP * HD, GROUP * HD), GROUP * HD)
        one = pl.ds(pl.multiple_of(head * HD, HD), HD)
        moves = [
            (k_prev.at[:, one], k_buf.at[h, :rows]),
            (k_own.at[:, one], k_buf.at[h, rows:]),
            (q.at[:, wide], q_buf.at[h]),
            (v_prev.at[:, one], v_buf.at[h, :rows]),
            (v_own.at[:, one], v_buf.at[h, rows:]),
            (g.at[:, wide], g_buf.at[h]),
        ]
        for n, (source, target) in enumerate(moves):
            copy = pltpu.make_async_copy(source, target, sems.at[6 * h + n])
            copy.start()
            waits[h].append(copy)
    length_copy.wait()
    base = lax.axis_index("seq") * rows
    query_pos = base + lax.broadcasted_iota(jnp.int32, (1, rows), 1)
    start = jnp.zeros((1, rows), jnp.int32)
    end = jnp.int32(0)
    for d in range(ends.shape[1]):
        end = end + ends[0, d]
        start = jnp.where(end <= query_pos, end, start)
    key_pos = base - rows + lax.broadcasted_iota(jnp.int32, (2 * rows, rows), 0)
    visible = (key_pos >= start) & (key_pos <= query_pos)
    hidden = jnp.where(visible, 0.0, NEG_FILL).astype(F32)
    for n in range(pair):
        bias[:, n * rows : (n + 1) * rows] = hidden

    scale = 1.0 / math.sqrt(HD)
    scale2 = scale * math.log2(math.e)
    nt = (((1,), (1,)), ((), ()))
    nn = (((1,), (0,)), ((), ()))
    for r in range(heads):
        for copy in waits[r]:
            copy.wait()
        key, value = k_buf[r], v_buf[r]
        total = None
        for h in range(0, GROUP, pair):
            cols = [slice((h + n) * HD, (h + n + 1) * HD) for n in range(pair)]
            q_rows = jnp.concatenate([q_buf[r, :, c] for c in cols], axis=0)
            g_rows = jnp.concatenate([g_buf[r, :, c] for c in cols], axis=0)
            scores = lax.dot_general(key, q_rows, nt, preferred_element_type=F32)
            weights = lax.dot_general(value, g_rows, nt, preferred_element_type=F32)
            scores = scores * scale2 + bias[...]
            exponent = jnp.exp2(scores - jnp.max(scores, axis=0, keepdims=True))
            inverse = 1.0 / jnp.sum(exponent, axis=0, keepdims=True)
            delta = jnp.sum(exponent * weights, axis=0, keepdims=True) * inverse
            grads = ((exponent * (inverse * scale)) * (weights - delta)).astype(BF16)
            part = lax.dot_general(grads, q_rows, nn, preferred_element_type=F32)
            total = part if total is None else total + part
        outs[r // HALF][r % HALF] = total.astype(outs[0].dtype)


def attention(turn, lengths, q, g, k_prev, k_own, v_prev, v_own, dtype):
    rows = q.shape[0]
    heads = KVH
    size = heads * 2 * rows * GROUP * rows
    return pl.pallas_call(
        functools.partial(attention_kernel, turn),
        in_specs=[pl.BlockSpec(memory_space=pl.ANY)] * 7,
        out_specs=[pl.BlockSpec(memory_space=pltpu.VMEM)] * 2,
        out_shape=[jax.ShapeDtypeStruct((HALF, 2 * rows, HD), dtype)] * 2,
        scratch_shapes=[
            pltpu.SMEM(lengths.shape, jnp.int32),
            pltpu.VMEM((heads, rows, GROUP * HD), BF16),
            pltpu.VMEM((heads, rows, GROUP * HD), BF16),
            pltpu.VMEM((heads, 2 * rows, HD), BF16),
            pltpu.VMEM((heads, 2 * rows, HD), BF16),
            pltpu.VMEM((2 * rows, 4 * rows), F32),
            pltpu.SemaphoreType.DMA((6 * heads + 1,)),
        ],
        compiler_params=params(54),
        cost_estimate=cost(6 * size * HD, heads * rows * GROUP * HD * 4, size),
    )(lengths, q, g, k_prev, k_own, v_prev, v_own)


def pack_kernel(sizes, x_ref, *outs):
    ny, nz = sizes
    block = outs[0].shape[2] // CORES
    core, x, y, z_own = position()
    for m, out in enumerate(outs):
        for z in range(nz):
            for c in range(CORES):
                source = (((x ^ (m // ny)) * CORES + c) * nz + z) * ny + (y ^ (m % ny))
                at = pl.ds(pl.multiple_of(source * block, block), block)
                out[z, :, c * block : (c + 1) * block] = x_ref[:, at]


def pack(features, sizes):
    nx, ny, nz = sizes
    rows = features.shape[0]
    shape = jax.ShapeDtypeStruct((nz, rows, DW // (nx * ny * nz)), BF16)
    vmem = pl.BlockSpec(memory_space=pltpu.VMEM)
    return pl.pallas_call(
        functools.partial(pack_kernel, (ny, nz)),
        in_specs=[vmem],
        out_specs=[vmem] * (nx * ny),
        out_shape=[shape] * (nx * ny),
        compiler_params=params(),
        cost_estimate=cost(0, 64 << 20),
    )(features)


def merge_kernel(mine, theirs, *outs):
    rows = mine.shape[1] // 2
    core = position()[0]

    def write(even, odd):
        for h in range(HALF):
            out = outs[h]
            out[:rows] = even[h, :rows]
            total = even[h, rows:].astype(F32) + odd[h, :rows].astype(F32)
            out[rows : 2 * rows] = total.astype(BF16)
            out[2 * rows :] = odd[h, rows:]

    @pl.when(core == 0)
    def _():
        write(mine, theirs)

    @pl.when(core == 1)
    def _():
        write(theirs, mine)


def merge(mine, theirs):
    rows = mine.shape[1] // 2
    vmem = pl.BlockSpec(memory_space=pltpu.VMEM)
    return pl.pallas_call(
        merge_kernel,
        in_specs=[vmem, vmem],
        out_specs=[vmem] * HALF,
        out_shape=[jax.ShapeDtypeStruct((3 * rows, HD), BF16)] * HALF,
        compiler_params=params(),
        cost_estimate=cost(rows * WIDE, 7 * rows * WIDE * 2),
    )(mine, theirs)


def weight_kernel(nz, order, *refs):
    chips = [refs[order.index(m)] for m in range(4)]
    f_same = (refs[4], refs[5], refs[6], refs[7])
    f_other = [refs[8].at[m] for m in range(4)]
    sends, (keep, key_mine, key_theirs, same, other) = refs[9 : 8 + nz], refs[8 + nz :]
    rows = chips[0].shape[0] // 3
    core, x, y, z = position()
    for m in range(4):
        even = chips[m][rows : 2 * rows]
        odd = (chips[m][2 * rows :].astype(F32) + chips[m ^ 2][:rows].astype(F32)).astype(BF16)
        own = jnp.where(core == 0, even, odd)
        far = jnp.where(core == 0, odd, even)
        same[m * rows : (m + 1) * rows] = own
        other[m * rows : (m + 1) * rows] = far
        if m == 0:
            key_mine[...] = own
            key_theirs[...] = far
    tn = (((0,), (0,)), ((), ()))
    for m in (2, 3, 1, 0):
        left = jnp.concatenate([f[z ^ m] for f in f_same], axis=0)
        right = jnp.concatenate([f[z ^ m] for f in f_other], axis=0)
        product = lax.dot_general(same[...], left, tn, preferred_element_type=F32)
        product += lax.dot_general(other[...], right, tn, preferred_element_type=F32)
        if m == 0:
            keep[...] = product
        else:
            sends[m - 1][...] = product.astype(BF16)


def weight(order, chips, f_same, f_other):
    rows = chips[0].shape[0] // 3
    nz = f_same[0].shape[0]
    vmem = pl.BlockSpec(memory_space=pltpu.VMEM)
    square = (HD, f_same[0].shape[2])
    shapes = [jax.ShapeDtypeStruct(square, BF16)] * (nz - 1)
    shapes += [jax.ShapeDtypeStruct(square, F32)] + [jax.ShapeDtypeStruct((rows, HD), BF16)] * 2
    return pl.pallas_call(
        functools.partial(weight_kernel, nz, order),
        in_specs=[vmem] * 9,
        out_specs=[vmem] * len(shapes),
        out_shape=shapes,
        scratch_shapes=[pltpu.VMEM((4 * rows, HD), BF16)] * 2,
        compiler_params=params(),
        cost_estimate=cost(2 * 8 * rows * HD * 4 * WIDE, 4 << 20),
    )(*[chips[m] for m in order], *[f_same[m] for m in (0, 1, 2, 3)], *f_other)


def squares_kernel(*refs):
    squares = refs[-1]
    sums = 0.0
    for h in range(HALF):
        keep, r1, r2, r3 = refs[4 * h : 4 * h + 4]
        total = keep[...] + r1[...].astype(F32) + r2[...].astype(F32) + r3[...].astype(F32)
        half = total.shape[1] // 2
        low, high = total[:, :half], total[:, half:]
        sums += jnp.sum(low * low + high * high, axis=0, keepdims=True)
    squares[...] = jnp.broadcast_to(sums[None], squares.shape)


def plane_squares(parts, devices):
    cols, both = parts[0].shape
    vmem = pl.BlockSpec(memory_space=pltpu.VMEM)
    return pl.pallas_call(
        squares_kernel,
        in_specs=[vmem] * len(parts),
        out_specs=vmem,
        out_shape=jax.ShapeDtypeStruct((devices, 1, both // 2), F32),
        compiler_params=params(),
        cost_estimate=cost(16 * cols * both, cols * both * 20),
    )(*parts)


def rows_kernel(*refs):
    keys, (mine, theirs) = refs[4 * HALF : 5 * HALF], refs[-2:]
    core = position()[0]
    for h in range(HALF):
        keep, r1, r2, r3 = refs[4 * h : 4 * h + 4]
        total = keep[...] + r1[...].astype(F32) + r2[...].astype(F32) + r3[...].astype(F32)
        half = total.shape[1] // 2
        low, high = total[:, :half].T, total[:, half:].T
        cols = slice(h * HD, (h + 1) * HD)
        mine[:, cols] = jnp.where(core == 0, low, high)
        theirs[:, cols] = jnp.where(core == 0, high, low)
        theirs[:, WIDE + h * HD : WIDE + (h + 1) * HD] = keys[h][...].astype(F32)


def plane_rows(parts, keys):
    cols, both = parts[0].shape
    vmem = pl.BlockSpec(memory_space=pltpu.VMEM)
    return pl.pallas_call(
        rows_kernel,
        in_specs=[vmem] * (len(parts) + len(keys)),
        out_specs=[vmem] * 2,
        out_shape=[jax.ShapeDtypeStruct((both // 2, n * WIDE), F32) for n in (1, 2)],
        compiler_params=params(),
        cost_estimate=cost(16 * cols * both, cols * both * 28),
    )(*parts, *keys)


def join_kernel(mine, theirs, *refs):
    keys, (out, key_out) = refs[:HALF], refs[HALF:]
    first = position()[0] == 0
    rows, far = theirs[:, :WIDE], theirs[:, WIDE:].astype(BF16)
    key = jnp.concatenate([k[...] for k in keys], axis=1)
    out[:, :WIDE] = jnp.where(first, mine[...], rows)
    out[:, WIDE:] = jnp.where(first, rows, mine[...])
    key_out[0, :, :WIDE] = jnp.where(first, key, far)
    key_out[0, :, WIDE:] = jnp.where(first, far, key)


def join(mine, theirs, keys):
    rows = keys[0].shape[0]
    vmem = pl.BlockSpec(memory_space=pltpu.VMEM)
    return pl.pallas_call(
        join_kernel,
        in_specs=[vmem] * (2 + HALF),
        out_specs=[vmem] * 2,
        out_shape=[
            jax.ShapeDtypeStruct((mine.shape[0], KVH * HD), F32),
            jax.ShapeDtypeStruct((1, rows, KVH * HD), BF16),
        ],
        compiler_params=params(),
        cost_estimate=cost(0, 12 * rows * KVH * HD),
    )(mine, theirs, *keys)


def clip_kernel(squares, rows, out):
    entries = DW * KVH * HD
    total = jnp.sum(jnp.sum(squares[...], axis=0, keepdims=True), axis=2, keepdims=True)
    root_mean = jnp.sqrt(total / entries + 1e-06)
    out[...] = rows[...] * jnp.minimum(1.0, 1.0 / root_mean)[0]


def clip(squares, rows):
    vmem = pl.BlockSpec(memory_space=pltpu.VMEM)
    return pl.pallas_call(
        clip_kernel,
        in_specs=[vmem] * 2,
        out_specs=vmem,
        out_shape=jax.ShapeDtypeStruct(rows.shape, F32),
        compiler_params=params(),
        cost_estimate=cost(rows.size, 8 * rows.size),
    )(squares, rows)


def planes(queries, keys, values, grad_out, features, doc_lengths):
    seq_count, dp_count = lax.axis_size("seq"), lax.axis_size("dp")
    devices = seq_count * dp_count
    nx, ny = seq_count // CORES, 2
    nz = dp_count // ny

    def swap(array, mask):
        return lax.ppermute(array, AXES, [(i, i ^ mask) for i in range(devices)])

    core_mask, x_mask, y_mask, z_mask = dp_count, CORES * dp_count, 1, ny
    following = [(i, (i + 1) % seq_count) for i in range(seq_count)]
    k_own, v_own = keys[0], values[0]
    k_prev = lax.ppermute(k_own, "seq", following)
    v_prev = lax.ppermute(v_own, "seq", following)

    masks = [0, y_mask, x_mask, x_mask + y_mask]
    packed = pack(features[0], (nx, ny, nz))
    f_same = [packed[0]] + [swap(part, mask) for part, mask in zip(packed[1:], masks[1:])]

    near = (queries[0], grad_out[0], k_prev, k_own, v_prev, v_own)
    to_send, mine = attention(True, doc_lengths, *near, BF16)
    theirs = swap(to_send, core_mask)
    pieces = merge(mine, theirs)
    f_ready, _ = lax.optimization_barrier((f_same, pieces[0]))
    far, late = lax.optimization_barrier((swap(jnp.stack(f_ready), core_mask), pieces[1]))
    f_other = [far]
    chips = [[piece] + [swap(piece, mask) for mask in masks[1:]] for piece in (pieces[0], late)]

    parts, keys_mine, keys_send = [], [], []
    for h in range(HALF):
        *sends, keep, key_mine, key_send = weight(ORDER[h], chips[h], f_same, f_other)
        parts += [keep] + [swap(sends[m], (m + 1) * z_mask) for m in SUMS[h]]
        keys_mine.append(key_mine)
        keys_send.append(key_send)
    squares = plane_squares(parts, devices)
    parts[0], squares = lax.optimization_barrier((parts[0], squares))
    squares = lax.all_to_all(squares, AXES, 0, 0, tiled=True)
    rows_mine, rows_send = plane_rows(parts, keys_send)
    rows_other = swap(rows_send, core_mask)
    rows, key_grad = join(rows_mine, rows_other, keys_mine)
    return key_grad, clip(squares, rows)


def rings(queries, keys, values, grad_out, features, doc_lengths):
    seq_count = lax.axis_size("seq")
    rows = queries.shape[1]
    following = [(i, (i + 1) % seq_count) for i in range(seq_count)]
    preceding = [(i, (i - 1) % seq_count) for i in range(seq_count)]
    k_own, v_own = keys[0], values[0]
    k_prev = lax.ppermute(k_own, "seq", following)
    v_prev = lax.ppermute(v_own, "seq", following)
    near = (queries[0], grad_out[0], k_prev, k_own, v_prev, v_own)
    parts = jnp.concatenate(attention(False, doc_lengths, *near, F32), axis=0)
    parts = parts.transpose(1, 0, 2).reshape(2 * rows, KVH * HD)
    after = lax.ppermute(parts[:rows], "seq", preceding)
    key_grad = (parts[rows:] + after).astype(BF16)
    columns = lax.all_to_all(features[0], "seq", split_axis=1, concat_axis=0, tiled=True)
    weight_part = lax.dot_general(
        columns,
        lax.all_gather(key_grad, "seq", axis=0, tiled=True),
        (((0,), (0,)), ((), ())),
        preferred_element_type=F32,
    )
    own_rows = lax.psum_scatter(weight_part, "dp", scatter_dimension=0, tiled=True)
    squares = lax.psum(jnp.sum(own_rows * own_rows), AXES)
    root_mean = jnp.sqrt(squares / (DW * KVH * HD) + 1e-06)
    return (key_grad[None], own_rows * jnp.minimum(1.0, 1.0 / root_mean))


def solution(mesh):
    in_specs = (
        P("dp", "seq", None),
        P("dp", "seq", None),
        P("dp", "seq", None),
        P("dp", "seq", None),
        P("dp", "seq", None),
        P("dp", None),
    )
    out_specs = (P("dp", "seq", None), P(("seq", "dp"), None))
    small = mesh.shape["seq"] == 2 * CORES and mesh.shape["dp"] == 8
    body = planes if small else rings
    return jax.shard_map(body, mesh=mesh, in_specs=in_specs, out_specs=out_specs, check_vma=False)
```

```python
import functools
import math

import jax
import jax.numpy as jnp
from jax import lax
from jax.experimental import pallas as pl
from jax.experimental.pallas import tpu as pltpu
from jax.sharding import PartitionSpec as P

HD = 128
HQ = 32
KVH = 4
DW = 4096
GROUP = HQ // KVH

NEG_FILL = -1e30
AXES = ("seq", "dp")
F32 = jnp.float32
BF16 = jnp.bfloat16
CORES = 2
ORDER = ((0, 2, 1, 3), (0, 2, 1, 3))
SUMS = ((2, 1, 0), (1, 2, 0))
HALF = KVH // CORES
WIDE = HALF * HD


def params(mib=40):
    return pltpu.CompilerParams(vmem_limit_bytes=mib << 20)


def cost(flops, moved, exps=0):
    return pl.CostEstimate(flops=flops, bytes_accessed=moved, transcendentals=exps)


def position():
    seq, dp = lax.axis_index("seq"), lax.axis_index("dp")
    return seq & 1, seq >> 1, dp & 1, dp >> 1


def attention_kernel(turn, lengths, q, g, k_prev, k_own, v_prev, v_own, *refs):
    outs, scratch = refs[:2], refs[2:]
    ends, q_buf, g_buf, k_buf, v_buf, bias, sems = scratch
    rows = q.shape[0]
    pair = bias.shape[1] // rows
    heads = KVH
    core = position()[0]
    first = (1 - core) * HALF if turn else 0
    waits = [[] for _ in range(heads)]
    length_copy = pltpu.make_async_copy(lengths, ends, sems.at[6 * heads])
    length_copy.start()
    for h in range(heads):
        head = (first + h) & (KVH - 1)
        wide = pl.ds(pl.multiple_of(head * GROUP * HD, GROUP * HD), GROUP * HD)
        one = pl.ds(pl.multiple_of(head * HD, HD), HD)
        moves = [
            (k_prev.at[:, one], k_buf.at[h, :rows]),
            (k_own.at[:, one], k_buf.at[h, rows:]),
            (q.at[:, wide], q_buf.at[h]),
            (v_prev.at[:, one], v_buf.at[h, :rows]),
            (v_own.at[:, one], v_buf.at[h, rows:]),
            (g.at[:, wide], g_buf.at[h]),
        ]
        for n, (source, target) in enumerate(moves):
            copy = pltpu.make_async_copy(source, target, sems.at[6 * h + n])
            copy.start()
            waits[h].append(copy)
    length_copy.wait()
    base = lax.axis_index("seq") * rows
    query_pos = base + lax.broadcasted_iota(jnp.int32, (1, rows), 1)
    start = jnp.zeros((1, rows), jnp.int32)
    end = jnp.int32(0)
    for d in range(ends.shape[1]):
        end = end + ends[0, d]
        start = jnp.where(end <= query_pos, end, start)
    key_pos = base - rows + lax.broadcasted_iota(jnp.int32, (2 * rows, rows), 0)
    visible = (key_pos >= start) & (key_pos <= query_pos)
    hidden = jnp.where(visible, 0.0, NEG_FILL).astype(F32)
    for n in range(pair):
        bias[:, n * rows : (n + 1) * rows] = hidden

    scale = 1.0 / math.sqrt(HD)
    scale2 = scale * math.log2(math.e)
    nt = (((1,), (1,)), ((), ()))
    nn = (((1,), (0,)), ((), ()))
    for r in range(heads):
        for copy in waits[r]:
            copy.wait()
        key, value = k_buf[r], v_buf[r]
        total = None
        for h in range(0, GROUP, pair):
            cols = [slice((h + n) * HD, (h + n + 1) * HD) for n in range(pair)]
            q_rows = jnp.concatenate([q_buf[r, :, c] for c in cols], axis=0)
            g_rows = jnp.concatenate([g_buf[r, :, c] for c in cols], axis=0)
            scores = lax.dot_general(key, q_rows, nt, preferred_element_type=F32)
            weights = lax.dot_general(value, g_rows, nt, preferred_element_type=F32)
            scores = scores * scale2 + bias[...]
            exponent = jnp.exp2(scores - jnp.max(scores, axis=0, keepdims=True))
            inverse = 1.0 / jnp.sum(exponent, axis=0, keepdims=True)
            delta = jnp.sum(exponent * weights, axis=0, keepdims=True) * inverse
            grads = ((exponent * (inverse * scale)) * (weights - delta)).astype(BF16)
            part = lax.dot_general(grads, q_rows, nn, preferred_element_type=F32)
            total = part if total is None else total + part
        outs[r // HALF][r % HALF] = total.astype(outs[0].dtype)


def attention(turn, lengths, q, g, k_prev, k_own, v_prev, v_own, dtype):
    rows = q.shape[0]
    heads = KVH
    size = heads * 2 * rows * GROUP * rows
    return pl.pallas_call(
        functools.partial(attention_kernel, turn),
        in_specs=[pl.BlockSpec(memory_space=pl.ANY)] * 7,
        out_specs=[pl.BlockSpec(memory_space=pltpu.VMEM)] * 2,
        out_shape=[jax.ShapeDtypeStruct((HALF, 2 * rows, HD), dtype)] * 2,
        scratch_shapes=[
            pltpu.SMEM(lengths.shape, jnp.int32),
            pltpu.VMEM((heads, rows, GROUP * HD), BF16),
            pltpu.VMEM((heads, rows, GROUP * HD), BF16),
            pltpu.VMEM((heads, 2 * rows, HD), BF16),
            pltpu.VMEM((heads, 2 * rows, HD), BF16),
            pltpu.VMEM((2 * rows, 4 * rows), F32),
            pltpu.SemaphoreType.DMA((6 * heads + 1,)),
        ],
        compiler_params=params(54),
        cost_estimate=cost(6 * size * HD, heads * rows * GROUP * HD * 4, size),
    )(lengths, q, g, k_prev, k_own, v_prev, v_own)


def pack_kernel(sizes, x_ref, *outs):
    ny, nz = sizes
    block = outs[0].shape[2] // CORES
    core, x, y, z_own = position()
    for m, out in enumerate(outs):
        for z in range(nz):
            for c in range(CORES):
                source = (((x ^ (m // ny)) * CORES + c) * nz + z) * ny + (y ^ (m % ny))
                at = pl.ds(pl.multiple_of(source * block, block), block)
                out[z, :, c * block : (c + 1) * block] = x_ref[:, at]


def pack(features, sizes):
    nx, ny, nz = sizes
    rows = features.shape[0]
    shape = jax.ShapeDtypeStruct((nz, rows, DW // (nx * ny * nz)), BF16)
    vmem = pl.BlockSpec(memory_space=pltpu.VMEM)
    return pl.pallas_call(
        functools.partial(pack_kernel, (ny, nz)),
        in_specs=[vmem],
        out_specs=[vmem] * (nx * ny),
        out_shape=[shape] * (nx * ny),
        compiler_params=params(),
        cost_estimate=cost(0, 64 << 20),
    )(features)


def merge_kernel(mine, theirs, *outs):
    rows = mine.shape[1] // 2
    core = position()[0]

    def write(even, odd):
        for h in range(HALF):
            out = outs[h]
            out[:rows] = even[h, :rows]
            total = even[h, rows:].astype(F32) + odd[h, :rows].astype(F32)
            out[rows : 2 * rows] = total.astype(BF16)
            out[2 * rows :] = odd[h, rows:]

    @pl.when(core == 0)
    def _():
        write(mine, theirs)

    @pl.when(core == 1)
    def _():
        write(theirs, mine)


def merge(mine, theirs):
    rows = mine.shape[1] // 2
    vmem = pl.BlockSpec(memory_space=pltpu.VMEM)
    return pl.pallas_call(
        merge_kernel,
        in_specs=[vmem, vmem],
        out_specs=[vmem] * HALF,
        out_shape=[jax.ShapeDtypeStruct((3 * rows, HD), BF16)] * HALF,
        compiler_params=params(),
        cost_estimate=cost(rows * WIDE, 7 * rows * WIDE * 2),
    )(mine, theirs)


def weight_kernel(nz, order, *refs):
    chips = [refs[order.index(m)] for m in range(4)]
    f_same = (refs[4], refs[5], refs[6], refs[7])
    f_other = [refs[8].at[m] for m in range(4)]
    sends, (keep, key_mine, key_theirs, same, other) = refs[9 : 8 + nz], refs[8 + nz :]
    rows = chips[0].shape[0] // 3
    core, x, y, z = position()
    for m in range(4):
        even = chips[m][rows : 2 * rows]
        odd = (chips[m][2 * rows :].astype(F32) + chips[m ^ 2][:rows].astype(F32)).astype(BF16)
        own = jnp.where(core == 0, even, odd)
        far = jnp.where(core == 0, odd, even)
        same[m * rows : (m + 1) * rows] = own
        other[m * rows : (m + 1) * rows] = far
        if m == 0:
            key_mine[...] = own
            key_theirs[...] = far
    tn = (((0,), (0,)), ((), ()))
    for m in (2, 3, 1, 0):
        left = jnp.concatenate([f[z ^ m] for f in f_same], axis=0)
        right = jnp.concatenate([f[z ^ m] for f in f_other], axis=0)
        product = lax.dot_general(same[...], left, tn, preferred_element_type=F32)
        product += lax.dot_general(other[...], right, tn, preferred_element_type=F32)
        if m == 0:
            keep[...] = product
        else:
            sends[m - 1][...] = product.astype(BF16)


def weight(order, chips, f_same, f_other):
    rows = chips[0].shape[0] // 3
    nz = f_same[0].shape[0]
    vmem = pl.BlockSpec(memory_space=pltpu.VMEM)
    square = (HD, f_same[0].shape[2])
    shapes = [jax.ShapeDtypeStruct(square, BF16)] * (nz - 1)
    shapes += [jax.ShapeDtypeStruct(square, F32)] + [jax.ShapeDtypeStruct((rows, HD), BF16)] * 2
    return pl.pallas_call(
        functools.partial(weight_kernel, nz, order),
        in_specs=[vmem] * 9,
        out_specs=[vmem] * len(shapes),
        out_shape=shapes,
        scratch_shapes=[pltpu.VMEM((4 * rows, HD), BF16)] * 2,
        compiler_params=params(),
        cost_estimate=cost(2 * 8 * rows * HD * 4 * WIDE, 4 << 20),
    )(*[chips[m] for m in order], *[f_same[m] for m in (0, 1, 2, 3)], *f_other)


def squares_kernel(*refs):
    squares = refs[-1]
    sums = 0.0
    for h in range(HALF):
        keep, r1, r2, r3 = refs[4 * h : 4 * h + 4]
        total = keep[...] + r1[...].astype(F32) + r2[...].astype(F32) + r3[...].astype(F32)
        half = total.shape[1] // 2
        low, high = total[:, :half], total[:, half:]
        sums += jnp.sum(low * low + high * high, axis=0, keepdims=True)
    squares[...] = jnp.broadcast_to(sums[None], squares.shape)


def plane_squares(parts, devices):
    cols, both = parts[0].shape
    vmem = pl.BlockSpec(memory_space=pltpu.VMEM)
    return pl.pallas_call(
        squares_kernel,
        in_specs=[vmem] * len(parts),
        out_specs=vmem,
        out_shape=jax.ShapeDtypeStruct((devices, 1, both // 2), F32),
        compiler_params=params(),
        cost_estimate=cost(16 * cols * both, cols * both * 20),
    )(*parts)


def rows_kernel(*refs):
    keys, (mine, theirs) = refs[4 * HALF : 5 * HALF], refs[-2:]
    core = position()[0]
    for h in range(HALF):
        keep, r1, r2, r3 = refs[4 * h : 4 * h + 4]
        total = keep[...] + r1[...].astype(F32) + r2[...].astype(F32) + r3[...].astype(F32)
        half = total.shape[1] // 2
        low, high = total[:, :half].T, total[:, half:].T
        cols = slice(h * HD, (h + 1) * HD)
        mine[:, cols] = jnp.where(core == 0, low, high)
        theirs[:, cols] = jnp.where(core == 0, high, low)
        theirs[:, WIDE + h * HD : WIDE + (h + 1) * HD] = keys[h][...].astype(F32)


def plane_rows(parts, keys):
    cols, both = parts[0].shape
    vmem = pl.BlockSpec(memory_space=pltpu.VMEM)
    return pl.pallas_call(
        rows_kernel,
        in_specs=[vmem] * (len(parts) + len(keys)),
        out_specs=[vmem] * 2,
        out_shape=[jax.ShapeDtypeStruct((both // 2, n * WIDE), F32) for n in (1, 2)],
        compiler_params=params(),
        cost_estimate=cost(16 * cols * both, cols * both * 28),
    )(*parts, *keys)


def join_kernel(mine, theirs, *refs):
    keys, (out, key_out) = refs[:HALF], refs[HALF:]
    first = position()[0] == 0
    rows, far = theirs[:, :WIDE], theirs[:, WIDE:].astype(BF16)
    key = jnp.concatenate([k[...] for k in keys], axis=1)
    out[:, :WIDE] = jnp.where(first, mine[...], rows)
    out[:, WIDE:] = jnp.where(first, rows, mine[...])
    key_out[0, :, :WIDE] = jnp.where(first, key, far)
    key_out[0, :, WIDE:] = jnp.where(first, far, key)


def join(mine, theirs, keys):
    rows = keys[0].shape[0]
    vmem = pl.BlockSpec(memory_space=pltpu.VMEM)
    return pl.pallas_call(
        join_kernel,
        in_specs=[vmem] * (2 + HALF),
        out_specs=[vmem] * 2,
        out_shape=[
            jax.ShapeDtypeStruct((mine.shape[0], KVH * HD), F32),
            jax.ShapeDtypeStruct((1, rows, KVH * HD), BF16),
        ],
        compiler_params=params(),
        cost_estimate=cost(0, 12 * rows * KVH * HD),
    )(mine, theirs, *keys)


def clip_kernel(squares, rows, out):
    entries = DW * KVH * HD
    total = jnp.sum(jnp.sum(squares[...], axis=0, keepdims=True), axis=2, keepdims=True)
    root_mean = jnp.sqrt(total / entries + 1e-06)
    out[...] = rows[...] * jnp.minimum(1.0, 1.0 / root_mean)[0]


def clip(squares, rows):
    vmem = pl.BlockSpec(memory_space=pltpu.VMEM)
    return pl.pallas_call(
        clip_kernel,
        in_specs=[vmem] * 2,
        out_specs=vmem,
        out_shape=jax.ShapeDtypeStruct(rows.shape, F32),
        compiler_params=params(),
        cost_estimate=cost(rows.size, 8 * rows.size),
    )(squares, rows)


def planes(queries, keys, values, grad_out, features, doc_lengths):
    seq_count, dp_count = lax.axis_size("seq"), lax.axis_size("dp")
    devices = seq_count * dp_count
    nx, ny = seq_count // CORES, 2
    nz = dp_count // ny

    def swap(array, mask):
        return lax.ppermute(array, AXES, [(i, i ^ mask) for i in range(devices)])

    core_mask, x_mask, y_mask, z_mask = dp_count, CORES * dp_count, 1, ny
    following = [(i, (i + 1) % seq_count) for i in range(seq_count)]
    k_own, v_own = keys[0], values[0]
    k_prev = lax.ppermute(k_own, "seq", following)
    v_prev = lax.ppermute(v_own, "seq", following)

    masks = [0, y_mask, x_mask, x_mask + y_mask]
    packed = pack(features[0], (nx, ny, nz))
    f_same = [packed[0]] + [swap(part, mask) for part, mask in zip(packed[1:], masks[1:])]

    near = (queries[0], grad_out[0], k_prev, k_own, v_prev, v_own)
    to_send, mine = attention(True, doc_lengths, *near, BF16)
    theirs = swap(to_send, core_mask)
    pieces = merge(mine, theirs)
    f_ready, _ = lax.optimization_barrier((f_same, pieces[0]))
    far, late = lax.optimization_barrier((swap(jnp.stack(f_ready), core_mask), pieces[1]))
    f_other = [far]
    chips = [[piece] + [swap(piece, mask) for mask in masks[1:]] for piece in (pieces[0], late)]

    parts, keys_mine, keys_send = [], [], []
    for h in range(HALF):
        *sends, keep, key_mine, key_send = weight(ORDER[h], chips[h], f_same, f_other)
        parts += [keep] + [swap(sends[m], (m + 1) * z_mask) for m in SUMS[h]]
        keys_mine.append(key_mine)
        keys_send.append(key_send)
    squares = plane_squares(parts, devices)
    parts[0], squares = lax.optimization_barrier((parts[0], squares))
    squares = lax.all_to_all(squares, AXES, 0, 0, tiled=True)
    rows_mine, rows_send = plane_rows(parts, keys_send)
    rows_other = swap(rows_send, core_mask)
    rows, key_grad = join(rows_mine, rows_other, keys_mine)
    return key_grad, clip(squares, rows)


def rings(queries, keys, values, grad_out, features, doc_lengths):
    seq_count = lax.axis_size("seq")
    rows = queries.shape[1]
    following = [(i, (i + 1) % seq_count) for i in range(seq_count)]
    preceding = [(i, (i - 1) % seq_count) for i in range(seq_count)]
    k_own, v_own = keys[0], values[0]
    k_prev = lax.ppermute(k_own, "seq", following)
    v_prev = lax.ppermute(v_own, "seq", following)
    near = (queries[0], grad_out[0], k_prev, k_own, v_prev, v_own)
    parts = jnp.concatenate(attention(False, doc_lengths, *near, F32), axis=0)
    parts = parts.transpose(1, 0, 2).reshape(2 * rows, KVH * HD)
    after = lax.ppermute(parts[:rows], "seq", preceding)
    key_grad = (parts[rows:] + after).astype(BF16)
    columns = lax.all_to_all(features[0], "seq", split_axis=1, concat_axis=0, tiled=True)
    weight_part = lax.dot_general(
        columns,
        lax.all_gather(key_grad, "seq", axis=0, tiled=True),
        (((0,), (0,)), ((), ())),
        preferred_element_type=F32,
    )
    own_rows = lax.psum_scatter(weight_part, "dp", scatter_dimension=0, tiled=True)
    squares = lax.psum(jnp.sum(own_rows * own_rows), AXES)
    root_mean = jnp.sqrt(squares / (DW * KVH * HD) + 1e-06)
    return (key_grad[None], own_rows * jnp.minimum(1.0, 1.0 / root_mean))


def solution(mesh):
    in_specs = (
        P("dp", "seq", None),
        P("dp", "seq", None),
        P("dp", "seq", None),
        P("dp", "seq", None),
        P("dp", "seq", None),
        P("dp", None),
    )
    out_specs = (P("dp", "seq", None), P(("seq", "dp"), None))
    small = mesh.shape["seq"] == 2 * CORES and mesh.shape["dp"] == 8
    body = planes if small else rings
    return jax.shard_map(body, mesh=mesh, in_specs=in_specs, out_specs=out_specs, check_vma=False)
```

```python
import functools
import math

import jax
import jax.numpy as jnp
from jax import lax
from jax.experimental import pallas as pl
from jax.experimental.pallas import tpu as pltpu
from jax.sharding import PartitionSpec as P

HD = 128
HQ = 32
KVH = 4
DW = 4096
GROUP = HQ // KVH

NEG_FILL = -1e30
AXES = ("seq", "dp")
F32 = jnp.float32
BF16 = jnp.bfloat16
CORES = 2
ORDER = ((0, 2, 1, 3), (0, 2, 1, 3))
SUMS = ((2, 1, 0), (2, 0, 1))
HALF = KVH // CORES
WIDE = HALF * HD


def params(mib=40):
    return pltpu.CompilerParams(vmem_limit_bytes=mib << 20)


def cost(flops, moved, exps=0):
    return pl.CostEstimate(flops=flops, bytes_accessed=moved, transcendentals=exps)


def position():
    seq, dp = lax.axis_index("seq"), lax.axis_index("dp")
    return seq & 1, seq >> 1, dp & 1, dp >> 1


def attention_kernel(turn, lengths, q, g, k_prev, k_own, v_prev, v_own, *refs):
    outs, scratch = refs[:2], refs[2:]
    ends, q_buf, g_buf, k_buf, v_buf, bias, sems = scratch
    rows = q.shape[0]
    pair = bias.shape[1] // rows
    heads = KVH
    core = position()[0]
    first = (1 - core) * HALF if turn else 0
    waits = [[] for _ in range(heads)]
    length_copy = pltpu.make_async_copy(lengths, ends, sems.at[6 * heads])
    length_copy.start()
    for h in range(heads):
        head = (first + h) & (KVH - 1)
        wide = pl.ds(pl.multiple_of(head * GROUP * HD, GROUP * HD), GROUP * HD)
        one = pl.ds(pl.multiple_of(head * HD, HD), HD)
        moves = [
            (k_prev.at[:, one], k_buf.at[h, :rows]),
            (k_own.at[:, one], k_buf.at[h, rows:]),
            (q.at[:, wide], q_buf.at[h]),
            (v_prev.at[:, one], v_buf.at[h, :rows]),
            (v_own.at[:, one], v_buf.at[h, rows:]),
            (g.at[:, wide], g_buf.at[h]),
        ]
        for n, (source, target) in enumerate(moves):
            copy = pltpu.make_async_copy(source, target, sems.at[6 * h + n])
            copy.start()
            waits[h].append(copy)
    length_copy.wait()
    base = lax.axis_index("seq") * rows
    query_pos = base + lax.broadcasted_iota(jnp.int32, (1, rows), 1)
    start = jnp.zeros((1, rows), jnp.int32)
    end = jnp.int32(0)
    for d in range(ends.shape[1]):
        end = end + ends[0, d]
        start = jnp.where(end <= query_pos, end, start)
    key_pos = base - rows + lax.broadcasted_iota(jnp.int32, (2 * rows, rows), 0)
    visible = (key_pos >= start) & (key_pos <= query_pos)
    hidden = jnp.where(visible, 0.0, NEG_FILL).astype(F32)
    for n in range(pair):
        bias[:, n * rows : (n + 1) * rows] = hidden

    scale = 1.0 / math.sqrt(HD)
    scale2 = scale * math.log2(math.e)
    nt = (((1,), (1,)), ((), ()))
    nn = (((1,), (0,)), ((), ()))
    for r in range(heads):
        for copy in waits[r]:
            copy.wait()
        key, value = k_buf[r], v_buf[r]
        total = None
        for h in range(0, GROUP, pair):
            cols = [slice((h + n) * HD, (h + n + 1) * HD) for n in range(pair)]
            q_rows = jnp.concatenate([q_buf[r, :, c] for c in cols], axis=0)
            g_rows = jnp.concatenate([g_buf[r, :, c] for c in cols], axis=0)
            scores = lax.dot_general(key, q_rows, nt, preferred_element_type=F32)
            weights = lax.dot_general(value, g_rows, nt, preferred_element_type=F32)
            scores = scores * scale2 + bias[...]
            exponent = jnp.exp2(scores - jnp.max(scores, axis=0, keepdims=True))
            inverse = 1.0 / jnp.sum(exponent, axis=0, keepdims=True)
            delta = jnp.sum(exponent * weights, axis=0, keepdims=True) * inverse
            grads = ((exponent * (inverse * scale)) * (weights - delta)).astype(BF16)
            part = lax.dot_general(grads, q_rows, nn, preferred_element_type=F32)
            total = part if total is None else total + part
        outs[r // HALF][r % HALF] = total.astype(outs[0].dtype)


def attention(turn, lengths, q, g, k_prev, k_own, v_prev, v_own, dtype):
    rows = q.shape[0]
    heads = KVH
    size = heads * 2 * rows * GROUP * rows
    return pl.pallas_call(
        functools.partial(attention_kernel, turn),
        in_specs=[pl.BlockSpec(memory_space=pl.ANY)] * 7,
        out_specs=[pl.BlockSpec(memory_space=pltpu.VMEM)] * 2,
        out_shape=[jax.ShapeDtypeStruct((HALF, 2 * rows, HD), dtype)] * 2,
        scratch_shapes=[
            pltpu.SMEM(lengths.shape, jnp.int32),
            pltpu.VMEM((heads, rows, GROUP * HD), BF16),
            pltpu.VMEM((heads, rows, GROUP * HD), BF16),
            pltpu.VMEM((heads, 2 * rows, HD), BF16),
            pltpu.VMEM((heads, 2 * rows, HD), BF16),
            pltpu.VMEM((2 * rows, 4 * rows), F32),
            pltpu.SemaphoreType.DMA((6 * heads + 1,)),
        ],
        compiler_params=params(54),
        cost_estimate=cost(6 * size * HD, heads * rows * GROUP * HD * 4, size),
    )(lengths, q, g, k_prev, k_own, v_prev, v_own)


def pack_kernel(sizes, x_ref, *outs):
    ny, nz = sizes
    block = outs[0].shape[2] // CORES
    core, x, y, z_own = position()
    for m, out in enumerate(outs):
        for z in range(nz):
            for c in range(CORES):
                source = (((x ^ (m // ny)) * CORES + c) * nz + z) * ny + (y ^ (m % ny))
                at = pl.ds(pl.multiple_of(source * block, block), block)
                out[z, :, c * block : (c + 1) * block] = x_ref[:, at]


def pack(features, sizes):
    nx, ny, nz = sizes
    rows = features.shape[0]
    shape = jax.ShapeDtypeStruct((nz, rows, DW // (nx * ny * nz)), BF16)
    vmem = pl.BlockSpec(memory_space=pltpu.VMEM)
    return pl.pallas_call(
        functools.partial(pack_kernel, (ny, nz)),
        in_specs=[vmem],
        out_specs=[vmem] * (nx * ny),
        out_shape=[shape] * (nx * ny),
        compiler_params=params(),
        cost_estimate=cost(0, 64 << 20),
    )(features)


def merge_kernel(mine, theirs, *outs):
    rows = mine.shape[1] // 2
    core = position()[0]

    def write(even, odd):
        for h in range(HALF):
            out = outs[h]
            out[:rows] = even[h, :rows]
            total = even[h, rows:].astype(F32) + odd[h, :rows].astype(F32)
            out[rows : 2 * rows] = total.astype(BF16)
            out[2 * rows :] = odd[h, rows:]

    @pl.when(core == 0)
    def _():
        write(mine, theirs)

    @pl.when(core == 1)
    def _():
        write(theirs, mine)


def merge(mine, theirs):
    rows = mine.shape[1] // 2
    vmem = pl.BlockSpec(memory_space=pltpu.VMEM)
    return pl.pallas_call(
        merge_kernel,
        in_specs=[vmem, vmem],
        out_specs=[vmem] * HALF,
        out_shape=[jax.ShapeDtypeStruct((3 * rows, HD), BF16)] * HALF,
        compiler_params=params(),
        cost_estimate=cost(rows * WIDE, 7 * rows * WIDE * 2),
    )(mine, theirs)


def weight_kernel(nz, order, *refs):
    chips = [refs[order.index(m)] for m in range(4)]
    f_same = (refs[4], refs[5], refs[6], refs[7])
    f_other = [refs[8].at[m] for m in range(4)]
    sends, (keep, key_mine, key_theirs, same, other) = refs[9 : 8 + nz], refs[8 + nz :]
    rows = chips[0].shape[0] // 3
    core, x, y, z = position()
    for m in range(4):
        even = chips[m][rows : 2 * rows]
        odd = (chips[m][2 * rows :].astype(F32) + chips[m ^ 2][:rows].astype(F32)).astype(BF16)
        own = jnp.where(core == 0, even, odd)
        far = jnp.where(core == 0, odd, even)
        same[m * rows : (m + 1) * rows] = own
        other[m * rows : (m + 1) * rows] = far
        if m == 0:
            key_mine[...] = own
            key_theirs[...] = far
    tn = (((0,), (0,)), ((), ()))
    for m in (2, 3, 1, 0):
        left = jnp.concatenate([f[z ^ m] for f in f_same], axis=0)
        right = jnp.concatenate([f[z ^ m] for f in f_other], axis=0)
        product = lax.dot_general(same[...], left, tn, preferred_element_type=F32)
        product += lax.dot_general(other[...], right, tn, preferred_element_type=F32)
        if m == 0:
            keep[...] = product
        else:
            sends[m - 1][...] = product.astype(BF16)


def weight(order, chips, f_same, f_other):
    rows = chips[0].shape[0] // 3
    nz = f_same[0].shape[0]
    vmem = pl.BlockSpec(memory_space=pltpu.VMEM)
    square = (HD, f_same[0].shape[2])
    shapes = [jax.ShapeDtypeStruct(square, BF16)] * (nz - 1)
    shapes += [jax.ShapeDtypeStruct(square, F32)] + [jax.ShapeDtypeStruct((rows, HD), BF16)] * 2
    return pl.pallas_call(
        functools.partial(weight_kernel, nz, order),
        in_specs=[vmem] * 9,
        out_specs=[vmem] * len(shapes),
        out_shape=shapes,
        scratch_shapes=[pltpu.VMEM((4 * rows, HD), BF16)] * 2,
        compiler_params=params(),
        cost_estimate=cost(2 * 8 * rows * HD * 4 * WIDE, 4 << 20),
    )(*[chips[m] for m in order], *[f_same[m] for m in (0, 1, 2, 3)], *f_other)


def squares_kernel(*refs):
    squares = refs[-1]
    sums = 0.0
    for h in range(HALF):
        keep, r1, r2, r3 = refs[4 * h : 4 * h + 4]
        total = keep[...] + r1[...].astype(F32) + r2[...].astype(F32) + r3[...].astype(F32)
        half = total.shape[1] // 2
        low, high = total[:, :half], total[:, half:]
        sums += jnp.sum(low * low + high * high, axis=0, keepdims=True)
    squares[...] = jnp.broadcast_to(sums[None], squares.shape)


def plane_squares(parts, devices):
    cols, both = parts[0].shape
    vmem = pl.BlockSpec(memory_space=pltpu.VMEM)
    return pl.pallas_call(
        squares_kernel,
        in_specs=[vmem] * len(parts),
        out_specs=vmem,
        out_shape=jax.ShapeDtypeStruct((devices, 1, both // 2), F32),
        compiler_params=params(),
        cost_estimate=cost(16 * cols * both, cols * both * 20),
    )(*parts)


def rows_kernel(*refs):
    keys, (mine, theirs) = refs[4 * HALF : 5 * HALF], refs[-2:]
    core = position()[0]
    for h in range(HALF):
        keep, r1, r2, r3 = refs[4 * h : 4 * h + 4]
        total = keep[...] + r1[...].astype(F32) + r2[...].astype(F32) + r3[...].astype(F32)
        half = total.shape[1] // 2
        low, high = total[:, :half].T, total[:, half:].T
        cols = slice(h * HD, (h + 1) * HD)
        mine[:, cols] = jnp.where(core == 0, low, high)
        theirs[:, cols] = jnp.where(core == 0, high, low)
        theirs[:, WIDE + h * HD : WIDE + (h + 1) * HD] = keys[h][...].astype(F32)


def plane_rows(parts, keys):
    cols, both = parts[0].shape
    vmem = pl.BlockSpec(memory_space=pltpu.VMEM)
    return pl.pallas_call(
        rows_kernel,
        in_specs=[vmem] * (len(parts) + len(keys)),
        out_specs=[vmem] * 2,
        out_shape=[jax.ShapeDtypeStruct((both // 2, n * WIDE), F32) for n in (1, 2)],
        compiler_params=params(),
        cost_estimate=cost(16 * cols * both, cols * both * 28),
    )(*parts, *keys)


def join_kernel(mine, theirs, *refs):
    keys, (out, key_out) = refs[:HALF], refs[HALF:]
    first = position()[0] == 0
    rows, far = theirs[:, :WIDE], theirs[:, WIDE:].astype(BF16)
    key = jnp.concatenate([k[...] for k in keys], axis=1)
    out[:, :WIDE] = jnp.where(first, mine[...], rows)
    out[:, WIDE:] = jnp.where(first, rows, mine[...])
    key_out[0, :, :WIDE] = jnp.where(first, key, far)
    key_out[0, :, WIDE:] = jnp.where(first, far, key)


def join(mine, theirs, keys):
    rows = keys[0].shape[0]
    vmem = pl.BlockSpec(memory_space=pltpu.VMEM)
    return pl.pallas_call(
        join_kernel,
        in_specs=[vmem] * (2 + HALF),
        out_specs=[vmem] * 2,
        out_shape=[
            jax.ShapeDtypeStruct((mine.shape[0], KVH * HD), F32),
            jax.ShapeDtypeStruct((1, rows, KVH * HD), BF16),
        ],
        compiler_params=params(),
        cost_estimate=cost(0, 12 * rows * KVH * HD),
    )(mine, theirs, *keys)


def clip_kernel(squares, rows, out):
    entries = DW * KVH * HD
    total = jnp.sum(jnp.sum(squares[...], axis=0, keepdims=True), axis=2, keepdims=True)
    root_mean = jnp.sqrt(total / entries + 1e-06)
    out[...] = rows[...] * jnp.minimum(1.0, 1.0 / root_mean)[0]


def clip(squares, rows):
    vmem = pl.BlockSpec(memory_space=pltpu.VMEM)
    return pl.pallas_call(
        clip_kernel,
        in_specs=[vmem] * 2,
        out_specs=vmem,
        out_shape=jax.ShapeDtypeStruct(rows.shape, F32),
        compiler_params=params(),
        cost_estimate=cost(rows.size, 8 * rows.size),
    )(squares, rows)


def planes(queries, keys, values, grad_out, features, doc_lengths):
    seq_count, dp_count = lax.axis_size("seq"), lax.axis_size("dp")
    devices = seq_count * dp_count
    nx, ny = seq_count // CORES, 2
    nz = dp_count // ny

    def swap(array, mask):
        return lax.ppermute(array, AXES, [(i, i ^ mask) for i in range(devices)])

    core_mask, x_mask, y_mask, z_mask = dp_count, CORES * dp_count, 1, ny
    following = [(i, (i + 1) % seq_count) for i in range(seq_count)]
    k_own, v_own = keys[0], values[0]
    k_prev = lax.ppermute(k_own, "seq", following)
    v_prev = lax.ppermute(v_own, "seq", following)

    masks = [0, y_mask, x_mask, x_mask + y_mask]
    packed = pack(features[0], (nx, ny, nz))
    f_same = [packed[0]] + [swap(part, mask) for part, mask in zip(packed[1:], masks[1:])]

    near = (queries[0], grad_out[0], k_prev, k_own, v_prev, v_own)
    to_send, mine = attention(True, doc_lengths, *near, BF16)
    theirs = swap(to_send, core_mask)
    pieces = merge(mine, theirs)
    f_ready, _ = lax.optimization_barrier((f_same, pieces[0]))
    far, late = lax.optimization_barrier((swap(jnp.stack(f_ready), core_mask), pieces[1]))
    f_other = [far]
    chips = [[piece] + [swap(piece, mask) for mask in masks[1:]] for piece in (pieces[0], late)]

    parts, keys_mine, keys_send = [], [], []
    for h in range(HALF):
        *sends, keep, key_mine, key_send = weight(ORDER[h], chips[h], f_same, f_other)
        parts += [keep] + [swap(sends[m], (m + 1) * z_mask) for m in SUMS[h]]
        keys_mine.append(key_mine)
        keys_send.append(key_send)
    squares = plane_squares(parts, devices)
    parts[0], squares = lax.optimization_barrier((parts[0], squares))
    squares = lax.all_to_all(squares, AXES, 0, 0, tiled=True)
    rows_mine, rows_send = plane_rows(parts, keys_send)
    rows_other = swap(rows_send, core_mask)
    rows, key_grad = join(rows_mine, rows_other, keys_mine)
    return key_grad, clip(squares, rows)


def rings(queries, keys, values, grad_out, features, doc_lengths):
    seq_count = lax.axis_size("seq")
    rows = queries.shape[1]
    following = [(i, (i + 1) % seq_count) for i in range(seq_count)]
    preceding = [(i, (i - 1) % seq_count) for i in range(seq_count)]
    k_own, v_own = keys[0], values[0]
    k_prev = lax.ppermute(k_own, "seq", following)
    v_prev = lax.ppermute(v_own, "seq", following)
    near = (queries[0], grad_out[0], k_prev, k_own, v_prev, v_own)
    parts = jnp.concatenate(attention(False, doc_lengths, *near, F32), axis=0)
    parts = parts.transpose(1, 0, 2).reshape(2 * rows, KVH * HD)
    after = lax.ppermute(parts[:rows], "seq", preceding)
    key_grad = (parts[rows:] + after).astype(BF16)
    columns = lax.all_to_all(features[0], "seq", split_axis=1, concat_axis=0, tiled=True)
    weight_part = lax.dot_general(
        columns,
        lax.all_gather(key_grad, "seq", axis=0, tiled=True),
        (((0,), (0,)), ((), ())),
        preferred_element_type=F32,
    )
    own_rows = lax.psum_scatter(weight_part, "dp", scatter_dimension=0, tiled=True)
    squares = lax.psum(jnp.sum(own_rows * own_rows), AXES)
    root_mean = jnp.sqrt(squares / (DW * KVH * HD) + 1e-06)
    return (key_grad[None], own_rows * jnp.minimum(1.0, 1.0 / root_mean))


def solution(mesh):
    in_specs = (
        P("dp", "seq", None),
        P("dp", "seq", None),
        P("dp", "seq", None),
        P("dp", "seq", None),
        P("dp", "seq", None),
        P("dp", None),
    )
    out_specs = (P("dp", "seq", None), P(("seq", "dp"), None))
    small = mesh.shape["seq"] == 2 * CORES and mesh.shape["dp"] == 8
    body = planes if small else rings
    return jax.shard_map(body, mesh=mesh, in_specs=in_specs, out_specs=out_specs, check_vma=False)
```
